256 devices in a mesh: prow: 8 (over y, x_hi), pcol: 32 (over x_lo, z, core).
Axes of the slice: x: 4 (x_hi: 2, x_lo: 2; x = x_hi * 2 + x_lo), y: 4, z: 8, core: 2. Of those that a mesh axis runs over, the one named last changes fastest.
Arguments:
- top_inverse: float32 [24, 512, 24, 512], P(None, ('pcol', 'prow')), as said below
- normed_panel: float32 [2, 4, 512, 6144], P(None, None, 'pcol', 'prow'), may hold values from -0.125 to 0.125
- child_inverse: float32 [2, 6144, 6144], P(None, 'pcol', 'prow'), as said below
- structure: int32 [2, 4], replicated, may hold values from 0 to 23, as said below
Outputs:
- cross_cov: float32 [2, 4, 512, 6144], P(None, None, 'pcol', 'prow')
- child_cov: float32 [2, 6144, 6144], P(None, 'pcol', 'prow')
The draws below stay inside these ranges and needn't reach their ends.
Inputs may be any that keep to these rules, and one draw needn't show every extreme that they name: top_inverse is symmetric: entry [a, u, b, v] equals entry [b, v, a, u]. child_inverse is symmetric in its last two dimensions. `structure`: each row lists 4 different block numbers in increasing order.
All inputs are finite; a program needn't handle non-finite values.
Results may differ from the reference program's by a relative error of at most 0.0001.
Values sent between devices are 32-bit elements; how exact they have to be, the bound alone decides.
A program may use at most 128 MiB of HBM per device.

```python
import math
import jax
import jax.numpy as jnp
from jax import lax

NA = 12288
BLK = 512
NC = 6144
NBS = 4
NBLK = 24
NS = 2048


def draw_top_inverse(key, part):
    key = jax.random.fold_in(key, 11)
    noise_key = jax.random.fold_in(key, 0)
    shape = (NBLK, BLK, NBLK, BLK)
    noise = jax.random.normal(noise_key, shape, jnp.float32)
    symmetric = 0.5 * (noise + jnp.transpose(noise, (2, 3, 0, 1)))
    row_index = lax.broadcasted_iota(jnp.int32, shape, 0) * BLK + lax.broadcasted_iota(jnp.int32, shape, 1)
    col_index = lax.broadcasted_iota(jnp.int32, shape, 2) * BLK + lax.broadcasted_iota(jnp.int32, shape, 3)
    identity = (row_index == col_index).astype(jnp.float32)
    base = identity + (1.0 - identity) * symmetric * (0.7 / math.sqrt(NA))
    return base


def draw_child_inverse(key, part):
    key = jax.random.fold_in(key, 23)
    shape = (2, NC, NC)
    noise = jax.random.normal(key, shape, jnp.float32)
    symmetric = 0.5 * (noise + jnp.swapaxes(noise, 1, 2))
    identity = (lax.broadcasted_iota(jnp.int32, shape, 1) == lax.broadcasted_iota(jnp.int32, shape, 2)).astype(jnp.float32)
    return identity + (1.0 - identity) * symmetric * (0.7 / math.sqrt(NC))


def draw_structure(key, part):
    key = jax.random.fold_in(key, 37)
    chosen_rows = []
    for child_index in range(2):
        scores = jax.random.permutation(jax.random.fold_in(key, child_index), NBLK).astype(jnp.int32) + 1
        forced = NBLK - 1 if child_index == 0 else 0
        scores = jnp.where(jnp.arange(NBLK, dtype=jnp.int32) == forced, 0, scores)
        picked = jnp.argsort(scores)[:NBS]
        chosen_rows.append(jnp.sort(picked).astype(jnp.int32))
    return jnp.stack(chosen_rows)


def levels(own_key, extent, shards, least, high):
    loudness, own = 1.0, jax.random.fold_in(own_key, 6)
    for dim, blocks in shards:
        steps = jnp.exp(jax.random.uniform(jax.random.fold_in(own, dim), (blocks,), jnp.float32, least / len(shards), high / len(shards)))
        loudness = loudness * jnp.repeat(steps, extent[dim] // blocks).reshape([-1 if axis == dim else 1 for axis in range(len(extent))])
    return loudness


def gaussian(stream_key, dims, deviation, most, cuts=(), kind=jnp.bfloat16):
    level = levels(stream_key, dims, cuts, -0.22, 0.18) if cuts else 1.0
    values = jax.random.normal(stream_key, dims, jnp.float32) * deviation * level
    return jnp.minimum(jnp.maximum(values, -most), most).astype(kind)


def setup_inputs(seed: int = 0) -> dict:
    key_of = jax.random.split(jax.random.key(seed), 5)
    top_inverse = draw_top_inverse(jax.random.fold_in(key_of[4], 71), 0)
    normed_panel = gaussian(key_of[1], (2, NBS, BLK, NC), NS ** -0.5, 0.125, ((2, 32), (3, 8)), jnp.float32)
    child_inverse = draw_child_inverse(jax.random.fold_in(key_of[4], 71), 0)
    structure = draw_structure(jax.random.fold_in(key_of[4], 71), 0)
    return {"top_inverse": top_inverse, "normed_panel": normed_panel, "child_inverse": child_inverse, "structure": structure}


def reference(top_inverse, normed_panel, child_inverse, structure):
    crosses = []
    covariances = []
    for child_index in range(2):
        chosen = structure[child_index]
        row_blocks = jnp.take(top_inverse, chosen, axis=0)
        sub_block = jnp.take(row_blocks, chosen, axis=2).reshape(NBS * BLK, NBS * BLK)
        factor = normed_panel[child_index].reshape(NBS * BLK, NC)
        cross_block = -jnp.dot(sub_block, factor, precision=lax.Precision.HIGHEST, preferred_element_type=jnp.float32)
        inner_sum = jnp.dot(factor.T, cross_block, precision=lax.Precision.HIGHEST, preferred_element_type=jnp.float32)
        covariances.append(child_inverse[child_index] - inner_sum)
        crosses.append(cross_block.reshape(NBS, BLK, NC))
    return jnp.stack(crosses), jnp.stack(covariances)
```

```python
import jax
import jax.numpy as jnp
from jax import lax
from jax.experimental import pallas as pl
from jax.experimental.pallas import tpu as pltpu
from jax.sharding import PartitionSpec as P

MESH = pl.DeviceIdType.MESH
F32, BF16 = jnp.float32, jnp.bfloat16
NCHUNK = 3
QUAD = ((0, 1), (1, 0), (1, 1))
PLANE = 8


def bit_xor(a, b):
    return lax.rem(a + b, 2)


def split(x):
    hi = x.astype(BF16)
    return hi, (x - hi.astype(F32)).astype(BF16)


def mm(a, b):
    return jnp.dot(a, b, preferred_element_type=F32)


def mm3(a_hi, a_lo, b_hi, b_lo):
    return mm(a_hi, b_hi) + (mm(a_hi, b_lo) + mm(a_lo, b_hi))


def kernel(structure, top, panel, inverse, cross, cov, sel, s_all, s_hi, s_lo, p_all, p_hi, p_lo,
           x_own, x_send, x_mid, x_all, g_own, g_in, c_in, ss, rs):
    row, col = lax.axis_index("prow"), lax.axis_index("pcol")
    child, z, core = lax.div(col, 16), lax.rem(lax.div(col, 2), 8), lax.rem(col, 2)

    def at(r, c, zz, j):
        return (r, (c * 8 + lax.rem(zz + 8, 8)) * 2 + j)

    def quad(d):
        return bit_xor(child, d[0]), bit_xor(core, d[1])

    counter = [0]

    def sems(count):
        base = counter[0]
        counter[0] += count
        return base

    pending = []

    def send(src, dst, index, device, own=None):
        out = index if own is None else own
        copy = pltpu.make_async_remote_copy(src, dst, ss.at[out], rs.at[index], device_id=device, device_id_type=MESH)
        copy.start()
        return copy

    def wait_recv(landing, index):
        pltpu.make_async_remote_copy(landing, landing, ss.at[index], rs.at[index], device_id=(row, col), device_id_type=MESH).wait_recv()

    sib = at(row, child, z, 1 - core)
    half, quarter = lax.div(row, 4), lax.rem(row, 4)
    m, s = lax.div(z, 2), lax.rem(z, 2)
    sw = bit_xor(half, s)
    e = lax.rem(quarter - m - 2 * half + 8, 4)
    mid_row = 4 * sw + 2 * lax.div(e, 2) + bit_xor(lax.rem(e, 2), sw)
    mid_self = mid_row == row
    sw2 = lax.div(row, 4)
    e2 = 2 * lax.div(quarter, 2) + bit_xor(lax.rem(quarter, 2), sw2)
    half2 = bit_xor(sw2, s)
    q2 = lax.rem(e2 + m + 2 * half2, 4)
    far_z = 2 * q2 + core
    far = at(row, child, far_z, half2)
    far_self = (far_z == z) & (half2 == core)
    half3 = core
    m3 = lax.rem(m - e2 - 2 * half3 + 8, 4)
    s3 = bit_xor(sw2, half3)
    from_z = 2 * m3 + s3
    from_core = s
    src_far = at(row, child, from_z, from_core)

    def piece_z(r, h):
        w = lax.div(r, 4)
        k = lax.rem(r, 4)
        ee = 2 * lax.div(k, 2) + bit_xor(lax.rem(k, 2), w)
        return 2 * lax.rem(m - ee - 2 * h + 8, 4) + bit_xor(w, h)

    barrier = pltpu.get_barrier_semaphore()

    def greet(device):
        pl.semaphore_signal(barrier, inc=1, device_id=device, device_id_type=MESH)

    for d in QUAD:
        greet(at(row, quad(d)[0], z, quad(d)[1]))
    greet(at(row, child, z + 1, core))
    greet(at(row, child, z - 1, core))
    for d in range(1, PLANE):
        greet((lax.rem(row + d, PLANE), col))

    @pl.when(jnp.logical_not(far_self))
    def _():
        greet(far)
        greet(src_far)

    for c in range(2):
        for a in range(4):
            for u in range(2):
                for b in range(4):
                    sel[c, 2 * a + u:2 * a + u + 1, 512 * b:512 * b + 512] = top[structure[c, a], u, pl.ds(structure[c, b], 1), :]

    pl.semaphore_wait(barrier, 12 + 2 * (1 - far_self.astype(jnp.int32)))

    i_quad = sems(3 * NCHUNK)

    def quad_send(n):
        for k, d in enumerate(QUAD):
            c2, j2 = quad(d)
            cols = pl.ds(pl.multiple_of(384 * j2 + 128 * n, 128), 128)
            pending.append(send(panel.at[c2, :, :, :, cols], p_all.at[n, :, z, :, child, pl.ds(pl.multiple_of(16 * core, 16), 16), :],
                                i_quad + 3 * n + k, at(row, c2, z, j2)))
        cols = pl.ds(pl.multiple_of(384 * core + 128 * n, 128), 128)
        p_all[n, :, z, :, child, pl.ds(pl.multiple_of(16 * core, 16), 16), :] = panel[child, :, :, :, cols]

    def quad_wait(n):
        for k, d in enumerate(QUAD):
            c2, j2 = quad(d)
            wait_recv(p_all.at[n, :, z, :, c2, pl.ds(pl.multiple_of(16 * j2, 16), 16), :], i_quad + 3 * n + k)

    i_sx = sems(1)
    mine = 2 * row + core
    quad_send(0)
    pending.append(send(sel.at[1 - child], s_all.at[mine, child], i_sx, at(row, 1 - child, z, core)))
    s_all[mine, child] = sel[child]
    quad_send(1)
    quad_send(2)

    i_right, i_left = sems(8 * NCHUNK), sems(8 * NCHUNK)

    def chunk(n, h, zz):
        return p_all.at[n, h, lax.rem(zz + 16, 8)]

    def right_wait(n, h, step):
        wait_recv(chunk(n, h, z - 1 - step), i_right + 8 * n + 4 * h + step)

    def left_wait(n, h, step):
        wait_recv(chunk(n, h, z + 1 + step), i_left + 8 * n + 4 * h + step)

    def ring(n, step):
        for h in range(2):
            if step < 3 or h == 0:
                if step:
                    right_wait(n, h, step - 1)
                piece = chunk(n, h, z - step)
                pending.append(send(piece, piece, i_right + 8 * n + 4 * h + step, at(row, child, z + 1, core)))
            if step < 3 or h == 1:
                if step:
                    left_wait(n, h, step - 1)
                piece = chunk(n, h, z + step)
                pending.append(send(piece, piece, i_left + 8 * n + 4 * h + step, at(row, child, z - 1, core)))

    def ring_end(n):
        right_wait(n, 1, 2)
        left_wait(n, 0, 2)
        right_wait(n, 0, 3)
        left_wait(n, 1, 3)
        for h in range(2):
            for zz in range(8):
                hi, lo = split(p_all[n, h, zz])
                p_hi[2 * h:2 * h + 2, :, zz, :, 128 * n:128 * n + 128] = hi
                p_lo[2 * h:2 * h + 2, :, zz, :, 128 * n:128 * n + 128] = lo

    def plane_send(buf, base):
        for d in range(1, PLANE):
            pending.append(send(buf.at[mine], buf.at[mine], base + d, (lax.rem(row + d, PLANE), col)))
        pending.append(send(buf.at[mine], buf.at[mine], base + 8, sib))

    def plane_pass(buf, base):
        for d in range(1, PLANE):
            slot = 2 * lax.rem(row - d + PLANE, PLANE) + core
            wait_recv(buf.at[slot], base + d)
            pending.append(send(buf.at[slot], buf.at[slot], base + 8 + d, sib))

    def plane_end(buf, base):
        for d in range(PLANE):
            wait_recv(buf.at[2 * lax.rem(row - d + PLANE, PLANE) + 1 - core], base + 8 + d)

    i_s = sems(16)
    i_x = [sems(16) for _ in range(NCHUNK)]
    i_mid, i_far = sems(NCHUNK), sems(NCHUNK)
    i_cross = sems(3 * NCHUNK)
    i_g, i_gs = sems(12), sems(6)

    def s_end():
        plane_pass(s_all, i_s)
        plane_end(s_all, i_s)
        pos = lax.broadcasted_iota(jnp.int32, (256, 256), 0)
        old = lax.broadcasted_iota(jnp.int32, (256, 256), 1)
        a, k, j, r, u = pos >> 6, (pos >> 5) & 1, (pos >> 4) & 1, (pos >> 1) & 7, pos & 1
        order = jnp.where(old == r * 32 + j * 16 + k * 8 + a * 2 + u, 1.0, 0.0).astype(BF16)
        hi, lo = split(s_all[...].reshape(256, 2048))
        s_hi[...] = mm(order, hi).astype(BF16)
        s_lo[...] = mm(order, lo).astype(BF16)

    def x_compute(n):
        cols = slice(128 * n, 128 * n + 128)
        b_hi = p_hi[:, :, :, :, cols].reshape(2048, 128)
        b_lo = p_lo[:, :, :, :, cols].reshape(2048, 128)
        x = -mm3(s_hi[...], s_lo[...], b_hi, b_lo)
        x_own[n] = x.reshape(4, 2, 32, 128)
        x_send[n] = x.T

        @pl.when(mid_self)
        def _():
            x_mid[n] = x_send[n]

        @pl.when(jnp.logical_not(mid_self))
        def _():
            send(x_send.at[n], x_mid.at[n], i_mid + n, (mid_row, col))

    def cross_send(n):
        for k, d in enumerate(QUAD):
            c2, j2 = quad(d)
            pending.append(send(x_own.at[n, :, c2, pl.ds(pl.multiple_of(16 * j2, 16), 16), :], c_in.at[child, core, n],
                                i_cross + 3 * n + k, at(row, c2, z, j2)))
        c_in[child, core, n] = x_own[n, :, child, pl.ds(pl.multiple_of(16 * core, 16), 16), :]

    def cross_end(n):
        for k, d in enumerate(QUAD):
            c2, j2 = quad(d)
            wait_recv(c_in.at[c2, j2, n], i_cross + 3 * n + k)

    def mid_pass(n):
        slot = 2 * row + half2

        @pl.when(jnp.logical_not(mid_self))
        def _():
            wait_recv(x_mid.at[n], i_mid + n)

        @pl.when(far_self)
        def _():
            x_all[n, mine] = x_mid[n]

        @pl.when(jnp.logical_not(far_self))
        def _():
            send(x_mid.at[n], x_all.at[n, slot], i_far + n, far)

    def far_pass(n):
        @pl.when(jnp.logical_not(far_self))
        def _():
            wait_recv(x_all.at[n, mine], i_far + n)
        plane_send(x_all.at[n], i_x[n])

    def g_compute(n):
        plane_pass(x_all.at[n], i_x[n])
        plane_end(x_all.at[n], i_x[n])
        for rel in range(2):
            h = bit_xor(child, rel)

            def step(r, acc):
                zz = piece_z(r, h)
                x_hi, x_lo = split(x_all[n, 2 * r + h])
                b_hi = p_hi[:, :, zz].reshape(256, 384)
                b_lo = p_lo[:, :, zz].reshape(256, 384)
                return acc + mm3(x_hi, x_lo, b_hi, b_lo)

            g_own[n, rel] = lax.fori_loop(0, PLANE, step, jnp.zeros((128, 384), F32))

    def unit(n, rel, i):
        return g_own.at[n, rel, pl.ds(64 * i, 64), :]

    def g_send(n):
        for i in range(2):
            t = 2 * n + i
            j2, k = t // 3, t % 3
            pending.append(send(unit(n, 1, i), g_in.at[child, core, k], i_g + 6 + 3 * core + k, at(row, 1 - child, z, j2), i_gs + t))

            @pl.when(core == j2)
            def _():
                g_in[child, core, k] = g_own[n, 0, 64 * i:64 * i + 64]

            @pl.when(core != j2)
            def _():
                send(unit(n, 0, i), g_in.at[child, core, k], i_g + 3 * core + k, sib)

    def g_end():
        for k in range(3):
            wait_recv(g_in.at[child, 1 - core, k], i_g + 3 * (1 - core) + k)
            for h in range(2):
                wait_recv(g_in.at[1 - child, h, k], i_g + 6 + 3 * h + k)

    quad_wait(0)
    ring(0, 0)
    wait_recv(s_all.at[mine, 1 - child], i_sx)
    plane_send(s_all, i_s)
    ring(0, 1)
    quad_wait(1)
    quad_wait(2)
    ring(0, 2)
    ring(0, 3)
    ring(1, 0)
    s_end()
    ring_end(0)
    x_compute(0)
    ring(1, 1)
    cross_send(0)
    mid_pass(0)
    ring(1, 2)
    far_pass(0)
    ring(1, 3)
    ring(2, 0)
    ring_end(1)
    x_compute(1)
    ring(2, 1)
    cross_send(1)
    mid_pass(1)
    ring(2, 2)
    far_pass(1)
    ring(2, 3)
    ring_end(2)
    x_compute(2)
    cross_send(2)
    mid_pass(2)
    g_compute(0)
    g_send(0)
    far_pass(2)
    g_compute(1)
    g_send(1)
    for n in range(NCHUNK):
        cross_end(n)
    for c in range(2):
        for h in range(2):
            for n in range(NCHUNK):
                cross[c, :, :, 384 * h + 128 * n:384 * h + 128 * n + 128] = c_in[c, h, n]
    g_compute(2)
    g_send(2)
    g_end()
    for c in range(2):
        for h in range(2):
            cov[c, :, 384 * h:384 * h + 384] = inverse[c, :, 384 * h:384 * h + 384] - g_in[c, h].reshape(192, 384)

    for copy in pending:
        copy.wait_send()

    def late(src, dst, index):
        pltpu.make_async_remote_copy(src, dst, ss.at[index], rs.at[index], device_id=(row, col), device_id_type=MESH).wait_send()

    for n in range(NCHUNK):
        @pl.when(jnp.logical_not(mid_self))
        def _():
            late(x_send.at[n], x_mid.at[n], i_mid + n)

        @pl.when(jnp.logical_not(far_self))
        def _():
            late(x_mid.at[n], x_all.at[n, mine], i_far + n)

        for i in range(2):
            t = 2 * n + i

            @pl.when(core != t // 3)
            def _():
                late(unit(n, 0, i), g_in.at[child, core, t % 3], i_g + 3 * core + t % 3)


N_SEMS = 9 + 1 + 48 + 16 + 48 + 6 + 9 + 12 + 6


def body(top_inverse, normed_panel, child_inverse, structure):
    vmem = pl.BlockSpec(memory_space=pltpu.VMEM)
    panel = normed_panel.reshape(2, 2, 2, 16, 768)
    return pl.pallas_call(
        kernel,
        out_shape=(jax.ShapeDtypeStruct((2, 4, 16, 768), F32), jax.ShapeDtypeStruct((2, 192, 768), F32)),
        in_specs=[pl.BlockSpec(memory_space=pltpu.SMEM), vmem, vmem, vmem],
        out_specs=(vmem, vmem),
        scratch_shapes=[
            pltpu.VMEM((2, 8, 2048), F32),
            pltpu.VMEM((16, 2, 8, 2048), F32),
            pltpu.VMEM((256, 2048), BF16),
            pltpu.VMEM((256, 2048), BF16),
            pltpu.VMEM((NCHUNK, 2, 8, 2, 2, 32, 128), F32),
            pltpu.VMEM((4, 2, 8, 32, 384), BF16),
            pltpu.VMEM((4, 2, 8, 32, 384), BF16),
            pltpu.VMEM((NCHUNK, 4, 2, 32, 128), F32),
            pltpu.VMEM((NCHUNK, 128, 256), F32),
            pltpu.VMEM((NCHUNK, 128, 256), F32),
            pltpu.VMEM((NCHUNK, 16, 128, 256), F32),
            pltpu.VMEM((NCHUNK, 2, 128, 384), F32),
            pltpu.VMEM((2, 2, 3, 64, 384), F32),
            pltpu.VMEM((2, 2, NCHUNK, 4, 16, 128), F32),
            pltpu.SemaphoreType.DMA((N_SEMS,)),
            pltpu.SemaphoreType.DMA((N_SEMS,)),
        ],
        compiler_params=pltpu.CompilerParams(collective_id=0, has_side_effects=True, vmem_limit_bytes=48 * 2**20),
        name="selected_inverse",
    )(structure, top_inverse, panel, child_inverse)


def solution(mesh):
    in_specs = (
        P(None, ("pcol", "prow"), None, None),
        P(None, None, "pcol", "prow"),
        P(None, "pcol", "prow"),
        P(),
    )
    out_specs = (P(None, None, "pcol", "prow"), P(None, "pcol", "prow"))
    return jax.shard_map(body, mesh=mesh, in_specs=in_specs, out_specs=out_specs, check_vma=False)
```

```python
import functools

import jax
import jax.numpy as jnp
from jax import lax
from jax.experimental import pallas as pl
from jax.experimental.pallas import tpu as pltpu
from jax.sharding import PartitionSpec as P

MESH = pl.DeviceIdType.MESH
F32, BF16 = jnp.float32, jnp.bfloat16
NCHUNK = 6
QUAD = ((0, 1), (1, 0), (1, 1))
PLANE = 8


def bit_xor(a, b):
    return lax.rem(a + b, 2)


def split(x):
    hi = x.astype(BF16)
    return hi, (x - hi.astype(F32)).astype(BF16)


def merge(a, b):
    lane = lax.broadcasted_iota(jnp.int32, a.shape, a.ndim - 1)
    return jnp.where(lane < 64, a, pltpu.roll(b, 64, a.ndim - 1))


def merge_high(a, b):
    lane = lax.broadcasted_iota(jnp.int32, a.shape, a.ndim - 1)
    return jnp.where(lane < 64, pltpu.roll(a, 64, a.ndim - 1), b)


def mm(a, b):
    return jnp.dot(a, b, preferred_element_type=F32)


def kernel(structure, top_hbm, panel_hbm, inverse_hbm, cross, cov, top, panel, packed, inverse, sel, s_all, s_cat, p_all, k_hi, k_lo, p_hi, p_lo,
           x_own, x_send, x_mid, x_all, x_cat, g_own, g_in, c_in, ss, rs, ls):
    row, col = lax.axis_index("prow"), lax.axis_index("pcol")
    child, z, core = lax.div(col, 16), lax.rem(lax.div(col, 2), 8), lax.rem(col, 2)

    def at(r, c, zz, j):
        return (r, (c * 8 + lax.rem(zz + 8, 8)) * 2 + j)

    def quad(d):
        return bit_xor(child, d[0]), bit_xor(core, d[1])

    counts = [0, 0]

    def sems(side, count=1):
        counts[side] += count
        return counts[side] - count

    def send(src, dst, out, into, device):
        pltpu.make_async_remote_copy(src, dst, ss.at[out], rs.at[into], device_id=device, device_id_type=MESH).start()

    def wait_send(ref, index):
        pltpu.make_async_remote_copy(ref, ref, ss.at[index], rs.at[0], device_id=(row, col), device_id_type=MESH).wait_send()

    def wait_recv(ref, index):
        pltpu.make_async_remote_copy(ref, ref, ss.at[0], rs.at[index], device_id=(row, col), device_id_type=MESH).wait_recv()

    sib = at(row, child, z, 1 - core)
    half, quarter = lax.div(row, 4), lax.rem(row, 4)
    m, s = lax.div(z, 2), lax.rem(z, 2)
    sw = bit_xor(half, s)
    e = lax.rem(quarter - m - 2 * half + 8, 4)
    mid_row = 4 * sw + 2 * lax.div(e, 2) + bit_xor(lax.rem(e, 2), sw)
    mid_self = mid_row == row
    sw2 = lax.div(row, 4)
    e2 = 2 * lax.div(quarter, 2) + bit_xor(lax.rem(quarter, 2), sw2)
    half2 = bit_xor(sw2, s)
    q2 = lax.rem(e2 + m + 2 * half2, 4)
    far_z = 2 * q2 + core
    far = at(row, child, far_z, half2)
    far_self = (far_z == z) & (half2 == core)
    half3 = core
    m3 = lax.rem(m - e2 - 2 * half3 + 8, 4)
    s3 = bit_xor(sw2, half3)
    from_z = 2 * m3 + s3
    from_core = s
    src_far = at(row, child, from_z, from_core)

    loads = [pltpu.make_async_copy(a, b, ls.at[i]) for i, (a, b) in enumerate(((panel_hbm, panel), (top_hbm, top), (inverse_hbm, inverse)))]
    for load in loads:
        load.start()
    barrier = pltpu.get_barrier_semaphore()

    def greet(device):
        pl.semaphore_signal(barrier, inc=1, device_id=device, device_id_type=MESH)

    for d in QUAD:
        greet(at(row, quad(d)[0], z, quad(d)[1]))
    greet(at(row, child, z + 1, core))
    greet(at(row, child, z - 1, core))
    for d in range(1, PLANE):
        greet((lax.rem(row + d, PLANE), col))
        greet(at(lax.rem(row + d, PLANE), 1 - child, z, core))

    @pl.when(jnp.logical_not(far_self))
    def _():
        greet(far)
        greet(src_far)

    loads[0].wait()
    for c in range(2):
        for j in range(2):
            for n in range(3):
                for b in range(2):
                    low = panel[c, 0, b, :, 384 * j + 128 * n:384 * j + 128 * n + 128]
                    high = panel[c, 1, b, :, 384 * j + 128 * n:384 * j + 128 * n + 128]
                    packed[c, j, 2 * n, b] = merge(low, high)
                    packed[c, j, 2 * n + 1, b] = merge_high(low, high)
    for t in range(NCHUNK):
        p_all[t, z, :, child, pl.ds(pl.multiple_of(16 * core, 16), 16), :] = packed[child, core, t]
    pl.semaphore_wait(barrier, 19 + 2 * (1 - far_self.astype(jnp.int32)))

    out_quad, in_quad = sems(0, 3), sems(1, 3)

    def quad_send(n):
        for k, d in enumerate(QUAD):
            c2, j2 = quad(d)
            send(packed.at[c2, j2, 2 * n:2 * n + 2], p_all.at[2 * n:2 * n + 2, z, :, child, pl.ds(pl.multiple_of(16 * core, 16), 16), :],
                 out_quad + k, in_quad + n, at(row, c2, z, j2))

    def quad_wait(n):
        wait_recv(packed.at[0, 0], in_quad + n)

    def select():
        loads[1].wait()
        for c in range(2):
            for a in range(4):
                for u in range(2):
                    for b in range(4):
                        sel[c, 2 * a + u:2 * a + u + 1, 512 * b:512 * b + 512] = top[structure[c, a], u, pl.ds(structure[c, b], 1), :]
        s_all[row, core, child] = sel[child]

    out_ring, in_ring = sems(0), sems(1, 4 * NCHUNK)

    def chunk(n, zz, part=None):
        ref = p_all.at[n, lax.rem(zz + 16, 8)]
        return ref if part is None else ref.at[part]

    def ring_wait(n, step):
        wait_recv(p_all.at[n, 0:2 if step < 3 else 1], in_ring + 4 * n + step)

    def ring(n, step):
        if step:
            ring_wait(n, step - 1)
        for side, part in ((1, 0), (-1, 1)):
            block = chunk(n, z - side * step, part if step == 3 else None)
            send(block, block, out_ring, in_ring + 4 * n + step, at(row, child, z + side, core))

    def ring_end(n):
        ring_wait(n, 3)
        for zz in range(8):
            k_hi[:, :, zz], k_lo[:, :, zz] = split(p_all[n, zz])
            if n % 2:
                even, odd = p_all[n - 1, zz], p_all[n, zz]
                for k, block in enumerate((merge(even, odd), merge_high(even, odd))):
                    hi, lo = split(block)
                    p_hi[2 * k:2 * k + 2, :, zz, :, 64 * n - 64:64 * n + 64] = hi
                    p_lo[2 * k:2 * k + 2, :, zz, :, 64 * n - 64:64 * n + 64] = lo

    y_up, y_down, y_far = lax.rem(row + 2, 8), lax.rem(row + 6, 8), lax.rem(row + 4, 8)
    x_far = row + 1 - 2 * lax.rem(row, 2)

    out_plane, in_plane = sems(0, 2), sems(1, 3 * NCHUNK)

    def plane_copy(u, k, r, to):
        send(x_all.at[u, r, core], x_all.at[u, r, core], out_plane, in_plane + 3 * u + k, (to, col))

    def plane_send(u):
        for to in (y_far, x_far, y_up, y_down):
            plane_copy(u, 0, row, to)

    def plane_pass(u):
        wait_recv(x_all.at[u, 0:4, 0], in_plane + 3 * u)
        plane_copy(u, 1, x_far, y_up)
        plane_copy(u, 1, x_far, y_down)
        plane_copy(u, 1, y_far, x_far)

    def plane_end(u):
        wait_recv(x_all.at[u, 0:3, 0], in_plane + 3 * u + 1)
        send(x_all.at[u, :, core], x_all.at[u, :, core], out_plane + 1, in_plane + 3 * u + 2, sib)

    def plane_wait(u):
        wait_recv(x_all.at[u, :, 0], in_plane + 3 * u + 2)

    out_mid, out_far, in_mid, in_far = sems(0), sems(0), sems(1, NCHUNK), sems(1, NCHUNK)
    out_cross, in_cross = sems(0, 3), sems(1, 3)
    out_g, in_g = sems(0, 2), sems(1, 2)
    out_s, in_s = sems(0, 3), sems(1, 3)

    def sel_send():
        select()
        for d in (4, 5, 3, 2, 6, 7, 1, 0):
            to = lax.rem(row + d, PLANE)
            if d:
                send(sel.at[child], s_all.at[row, core, child], out_s, in_s, (to, col))
            send(sel.at[1 - child], s_all.at[row, core, child], out_s + 1, in_s + 1, at(to, 1 - child, z, core))

    def sel_pass():
        wait_recv(s_all.at[0:7, 0, 0], in_s)
        wait_recv(s_all.at[:, 0, 0], in_s + 1)
        send(s_all.at[:, core], s_all.at[:, core], out_s + 2, in_s + 2, sib)

    def sel_end():
        wait_recv(s_all.at[:, 0], in_s + 2)

    def s_end():
        sel_pass()
        sel_end()
        pos = lax.broadcasted_iota(jnp.int32, (256, 256), 0)
        old = lax.broadcasted_iota(jnp.int32, (256, 256), 1)
        a, k, j, r, u = pos >> 6, (pos >> 5) & 1, (pos >> 4) & 1, (pos >> 1) & 7, pos & 1
        order = jnp.where(old == r * 32 + j * 16 + k * 8 + a * 2 + u, 1.0, 0.0).astype(BF16)
        hi, lo = split(s_all[...].reshape(256, 2048))
        s_cat[0:256] = mm(order, hi).astype(BF16)
        s_cat[256:512] = mm(order, lo).astype(BF16)

    def x_compute(n):
        b_hi, b_lo = k_hi[...].reshape(1024, 128), k_lo[...].reshape(1024, 128)
        parts = []
        for k in range(2):
            x = mm(s_cat[:, 1024 * k:1024 * k + 1024], b_hi)
            parts.append(x[0:256] + (x[256:512] + mm(s_cat[0:256, 1024 * k:1024 * k + 1024], b_lo)))
        x = -(parts[0] + pltpu.roll(parts[1], 64, 1))
        if n % 2:
            x_own[n // 2] = merge(x_own[n // 2].reshape(256, 128), x).reshape(4, 2, 32, 128)
        else:
            x_own[n // 2] = x.reshape(4, 2, 32, 128)
        x_send[n] = x.T[0:64]

        @pl.when(mid_self)
        def _():
            x_mid[n] = x_send[n]

        @pl.when(jnp.logical_not(mid_self))
        def _():
            send(x_send.at[n], x_mid.at[n], out_mid, in_mid + n, (mid_row, col))

    def cross_send(n):
        for k, d in enumerate(QUAD):
            c2, j2 = quad(d)
            send(x_own.at[n, :, c2, pl.ds(pl.multiple_of(16 * j2, 16), 16), :], c_in.at[child, core, n],
                 out_cross + k, in_cross + k, at(row, c2, z, j2))
        c_in[child, core, n] = x_own[n, :, child, pl.ds(pl.multiple_of(16 * core, 16), 16), :]

    def mid_pass(u):
        @pl.when(jnp.logical_not(mid_self))
        def _():
            wait_recv(x_mid.at[u], in_mid + u)

        @pl.when(far_self)
        def _():
            x_all[u, row, core] = x_mid[u]

        @pl.when(jnp.logical_not(far_self))
        def _():
            send(x_mid.at[u], x_all.at[u, row, half2], out_far, in_far + u, far)

    def far_pass(u):
        @pl.when(jnp.logical_not(far_self))
        def _():
            wait_recv(x_all.at[u, 0, 0], in_far + u)
        plane_send(u)

    def plane_slot(zz, h):
        w = bit_xor(h, zz % 2)
        ee = lax.rem(m - zz // 2 - 2 * h + 16, 4)
        return 4 * w + 2 * lax.div(ee, 2) + bit_xor(lax.rem(ee, 2), w)

    def g_compute(u):
        plane_wait(u)
        for rel in range(2):
            h = bit_xor(child, rel)
            for zz in range(8):
                x_hi, x_lo = split(x_all[u, plane_slot(zz, h), h])
                x_cat[64 * rel:64 * rel + 64, 256 * zz:256 * zz + 256] = x_hi
                x_cat[64 * rel + 128:64 * rel + 192, 256 * zz:256 * zz + 256] = x_lo
        b_hi = jnp.concatenate([p_hi[:, :, zz].reshape(256, 384) for zz in range(8)])
        g = mm(x_cat[...], b_hi)
        b_lo = jnp.concatenate([p_lo[:, :, zz].reshape(256, 384) for zz in range(8)])
        g = g[0:128] + (g[128:256] + mm(x_cat[0:128], b_lo))
        g_own[u] = g.reshape(2, 64, 384)

    def g_send(u):
        j2, k = u // 3, u % 3
        send(g_own.at[u, 1], g_in.at[child, core, k], out_g + 1, in_g + 1, at(row, 1 - child, z, j2))

        @pl.when(core == j2)
        def _():
            g_in[child, core, k] = g_own[u, 0]

        @pl.when(core != j2)
        def _():
            send(g_own.at[u, 0], g_in.at[child, core, k], out_g, in_g, sib)

    def cross_write():
        for k in range(3):
            wait_recv(c_in.at[0, 0], in_cross + k)
        for c in range(2):
            for h in range(2):
                for n in range(3):
                    cross[c, :, :, 384 * h + 128 * n:384 * h + 128 * n + 128] = c_in[c, h, n]

    def cov_write():
        loads[2].wait()
        wait_recv(g_in.at[0, 0], in_g)
        wait_recv(g_in.at[0], in_g + 1)
        for c in range(2):
            for h in range(2):
                cov[c, :, 384 * h:384 * h + 384] = inverse[c, :, 384 * h:384 * h + 384] - g_in[c, h].reshape(192, 384)

    quad_send(0)
    quad_send(1)
    quad_send(2)
    sel_send()
    quad_wait(0)
    ring(0, 0)
    ring(1, 0)
    quad_wait(1)
    ring(2, 0)
    ring(0, 1)
    ring(1, 1)
    ring(0, 2)
    ring(2, 1)
    ring(1, 2)
    ring(0, 3)
    quad_wait(2)
    ring(3, 0)
    ring(2, 2)
    ring(1, 3)
    ring(3, 1)
    ring(4, 0)
    s_end()
    ring_end(0)
    x_compute(0)
    ring(2, 3)
    ring(3, 2)
    ring_end(1)
    x_compute(1)
    ring(4, 1)
    ring(5, 0)
    mid_pass(0)
    mid_pass(1)
    ring(3, 3)
    ring(4, 2)
    ring_end(2)
    x_compute(2)
    cross_send(0)
    far_pass(0)
    ring(5, 1)
    ring(4, 3)
    mid_pass(2)
    far_pass(1)
    ring_end(3)
    x_compute(3)
    ring(5, 2)
    ring(5, 3)
    plane_pass(0)
    mid_pass(3)
    far_pass(2)
    cross_send(1)
    ring_end(4)
    x_compute(4)
    plane_pass(1)
    plane_end(0)
    mid_pass(4)
    far_pass(3)
    plane_pass(2)
    plane_end(1)
    ring_end(5)
    x_compute(5)
    far_pass(4)
    plane_pass(3)
    mid_pass(5)
    plane_end(2)
    g_compute(0)
    g_send(0)
    g_compute(1)
    g_send(1)
    plane_end(3)
    plane_pass(4)
    g_compute(2)
    g_send(2)
    far_pass(5)
    cross_send(2)
    g_compute(3)
    g_send(3)
    plane_end(4)
    plane_pass(5)
    g_compute(4)
    g_send(4)
    cross_write()
    plane_end(5)
    g_compute(5)
    g_send(5)
    cov_write()

    for k in range(3):
        wait_send(packed.at[0, 0], out_quad + k)
        wait_send(c_in.at[0, 0], out_cross + k)
    wait_send(s_all.at[0:7, 0, 0], out_s)
    wait_send(s_all.at[:, 0, 0], out_s + 1)
    wait_send(s_all.at[:, 0], out_s + 2)
    wait_send(p_all.at[:, 0:7], out_ring)
    wait_send(x_all.at[:, 0:7, 0], out_plane)
    wait_send(x_all.at[:, :, 0], out_plane + 1)
    wait_send(g_own.at[0:3, 0], out_g)
    wait_send(g_own.at[:, 0], out_g + 1)

    @pl.when(jnp.logical_not(mid_self))
    def _():
        wait_send(x_send, out_mid)

    @pl.when(jnp.logical_not(far_self))
    def _():
        wait_send(x_mid, out_far)


N_OUT, N_IN = 16, 65


def body(top_inverse, normed_panel, child_inverse, structure):
    vmem = pl.BlockSpec(memory_space=pltpu.VMEM)
    panel = normed_panel.reshape(2, 2, 2, 16, 768)
    return pl.pallas_call(
        kernel,
        out_shape=(jax.ShapeDtypeStruct((2, 4, 16, 768), F32), jax.ShapeDtypeStruct((2, 192, 768), F32)),
        in_specs=[pl.BlockSpec(memory_space=pltpu.SMEM)] + [pl.BlockSpec(memory_space=pl.ANY)] * 3,
        out_specs=(vmem, vmem),
        scratch_shapes=[
            pltpu.VMEM((24, 2, 24, 512), F32),
            pltpu.VMEM((2, 2, 2, 16, 768), F32),
            pltpu.VMEM((2, 2, 6, 2, 16, 128), F32),
            pltpu.VMEM((2, 192, 768), F32),
            pltpu.VMEM((2, 8, 2048), F32),
            pltpu.VMEM((8, 2, 2, 8, 2048), F32),
            pltpu.VMEM((512, 2048), BF16),
            pltpu.VMEM((NCHUNK, 8, 2, 2, 32, 128), F32),
            pltpu.VMEM((2, 2, 8, 32, 128), BF16),
            pltpu.VMEM((2, 2, 8, 32, 128), BF16),
            pltpu.VMEM((4, 2, 8, 32, 384), BF16),
            pltpu.VMEM((4, 2, 8, 32, 384), BF16),
            pltpu.VMEM((3, 4, 2, 32, 128), F32),
            pltpu.VMEM((NCHUNK, 64, 256), F32),
            pltpu.VMEM((NCHUNK, 64, 256), F32),
            pltpu.VMEM((NCHUNK, 8, 2, 64, 256), F32),
            pltpu.VMEM((256, 2048), BF16),
            pltpu.VMEM((NCHUNK, 2, 64, 384), F32),
            pltpu.VMEM((2, 2, 3, 64, 384), F32),
            pltpu.VMEM((2, 2, 3, 4, 16, 128), F32),
            pltpu.SemaphoreType.DMA((N_OUT,)),
            pltpu.SemaphoreType.DMA((N_IN,)),
            pltpu.SemaphoreType.DMA((3,)),
        ],
        compiler_params=pltpu.CompilerParams(collective_id=0, has_side_effects=True, vmem_limit_bytes=60 * 2**20),
        name="selected_inverse",
    )(structure, top_inverse, panel, child_inverse)


def solution(mesh):
    in_specs = (
        P(None, ("pcol", "prow"), None, None),
        P(None, None, "pcol", "prow"),
        P(None, "pcol", "prow"),
        P(),
    )
    out_specs = (P(None, None, "pcol", "prow"), P(None, "pcol", "prow"))
    return jax.shard_map(body, mesh=mesh, in_specs=in_specs, out_specs=out_specs, check_vma=False)
```

```python
import functools

import jax
import jax.numpy as jnp
from jax import lax
from jax.experimental import pallas as pl
from jax.experimental.pallas import tpu as pltpu
from jax.sharding import PartitionSpec as P

MESH = pl.DeviceIdType.MESH
F32, BF16 = jnp.float32, jnp.bfloat16
NCHUNK = 6
QUAD = ((0, 1), (1, 0), (1, 1))
PLANE = 8


def bit_xor(a, b):
    return lax.rem(a + b, 2)


def split(x):
    hi = x.astype(BF16)
    return hi, (x - hi.astype(F32)).astype(BF16)


def merge(a, b):
    lane = lax.broadcasted_iota(jnp.int32, a.shape, a.ndim - 1)
    return jnp.where(lane < 64, a, pltpu.roll(b, 64, a.ndim - 1))


def merge_high(a, b):
    lane = lax.broadcasted_iota(jnp.int32, a.shape, a.ndim - 1)
    return jnp.where(lane < 64, pltpu.roll(a, 64, a.ndim - 1), b)


def mm(a, b):
    return jnp.dot(a, b, preferred_element_type=F32)


def kernel(structure, top_hbm, panel_hbm, inverse_hbm, cross, cov, top, panel, packed, inverse, sel, s_all, s_cat, p_all, k_hi, k_lo, p_hi, p_lo,
           x_own, x_send, x_mid, x_all, x_cat, g_own, g_in, c_in, ss, rs, ls):
    row, col = lax.axis_index("prow"), lax.axis_index("pcol")
    child, z, core = lax.div(col, 16), lax.rem(lax.div(col, 2), 8), lax.rem(col, 2)

    def at(r, c, zz, j):
        return (r, (c * 8 + lax.rem(zz + 8, 8)) * 2 + j)

    def quad(d):
        return bit_xor(child, d[0]), bit_xor(core, d[1])

    counts = [0, 0]

    def sems(side, count=1):
        counts[side] += count
        return counts[side] - count

    def send(src, dst, out, into, device):
        pltpu.make_async_remote_copy(src, dst, ss.at[out], rs.at[into], device_id=device, device_id_type=MESH).start()

    def wait_send(ref, index):
        pltpu.make_async_remote_copy(ref, ref, ss.at[index], rs.at[0], device_id=(row, col), device_id_type=MESH).wait_send()

    def wait_recv(ref, index):
        pltpu.make_async_remote_copy(ref, ref, ss.at[0], rs.at[index], device_id=(row, col), device_id_type=MESH).wait_recv()

    sib = at(row, child, z, 1 - core)
    half, quarter = lax.div(row, 4), lax.rem(row, 4)
    m, s = lax.div(z, 2), lax.rem(z, 2)
    sw = bit_xor(half, s)
    e = lax.rem(quarter - m - 2 * half + 8, 4)
    mid_row = 4 * sw + 2 * lax.div(e, 2) + bit_xor(lax.rem(e, 2), sw)
    mid_self = mid_row == row
    sw2 = lax.div(row, 4)
    e2 = 2 * lax.div(quarter, 2) + bit_xor(lax.rem(quarter, 2), sw2)
    half2 = bit_xor(sw2, s)
    q2 = lax.rem(e2 + m + 2 * half2, 4)
    far_z = 2 * q2 + core
    far = at(row, child, far_z, half2)
    far_self = (far_z == z) & (half2 == core)
    half3 = core
    m3 = lax.rem(m - e2 - 2 * half3 + 8, 4)
    s3 = bit_xor(sw2, half3)
    from_z = 2 * m3 + s3
    from_core = s
    src_far = at(row, child, from_z, from_core)

    loads = [pltpu.make_async_copy(a, b, ls.at[i]) for i, (a, b) in enumerate(((panel_hbm, panel), (top_hbm, top), (inverse_hbm, inverse)))]
    for load in loads:
        load.start()
    barrier = pltpu.get_barrier_semaphore()

    def greet(device):
        pl.semaphore_signal(barrier, inc=1, device_id=device, device_id_type=MESH)

    for d in QUAD:
        greet(at(row, quad(d)[0], z, quad(d)[1]))
    greet(at(row, child, z + 1, core))
    greet(at(row, child, z - 1, core))
    for d in range(1, PLANE):
        greet((lax.rem(row + d, PLANE), col))
        greet(at(lax.rem(row + d, PLANE), 1 - child, z, core))

    @pl.when(jnp.logical_not(far_self))
    def _():
        greet(far)
        greet(src_far)

    loads[0].wait()
    for c in range(2):
        for j in range(2):
            for n in range(3):
                for b in range(2):
                    low = panel[c, 0, b, :, 384 * j + 128 * n:384 * j + 128 * n + 128]
                    high = panel[c, 1, b, :, 384 * j + 128 * n:384 * j + 128 * n + 128]
                    packed[c, j, 2 * n, b] = merge(low, high)
                    packed[c, j, 2 * n + 1, b] = merge_high(low, high)
    for t in range(NCHUNK):
        p_all[t, z, :, child, pl.ds(pl.multiple_of(16 * core, 16), 16), :] = packed[child, core, t]
    pl.semaphore_wait(barrier, 19 + 2 * (1 - far_self.astype(jnp.int32)))

    out_quad, in_quad = sems(0, 3), sems(1, 3)

    def quad_send(n):
        for k, d in enumerate(QUAD):
            c2, j2 = quad(d)
            send(packed.at[c2, j2, 2 * n:2 * n + 2], p_all.at[2 * n:2 * n + 2, z, :, child, pl.ds(pl.multiple_of(16 * core, 16), 16), :],
                 out_quad + k, in_quad + n, at(row, c2, z, j2))

    def quad_wait(n):
        wait_recv(packed.at[0, 0], in_quad + n)

    def select():
        loads[1].wait()
        for c in range(2):
            for a in range(4):
                for u in range(2):
                    for b in range(4):
                        sel[c, 2 * a + u:2 * a + u + 1, 512 * b:512 * b + 512] = top[structure[c, a], u, pl.ds(structure[c, b], 1), :]
        s_all[row, core, child] = sel[child]

    out_ring, in_ring = sems(0), sems(1, 4 * NCHUNK)

    def chunk(n, zz, part=None):
        ref = p_all.at[n, lax.rem(zz + 16, 8)]
        return ref if part is None else ref.at[part]

    def ring_wait(n, step):
        wait_recv(p_all.at[n, 0:2 if step < 3 else 1], in_ring + 4 * n + step)

    def ring(n, step):
        if step:
            ring_wait(n, step - 1)
        for side, part in ((1, 0), (-1, 1)):
            block = chunk(n, z - side * step, part if step == 3 else None)
            send(block, block, out_ring, in_ring + 4 * n + step, at(row, child, z + side, core))

    def ring_end(n):
        ring_wait(n, 3)
        for zz in range(8):
            k_hi[:, :, zz], k_lo[:, :, zz] = split(p_all[n, zz])

    def unpack(n):
        for zz in range(8):
            even, odd = p_all[2 * n, zz], p_all[2 * n + 1, zz]
            for k, block in enumerate((merge(even, odd), merge_high(even, odd))):
                hi, lo = split(block)
                p_hi[2 * k:2 * k + 2, :, zz, :, 128 * n:128 * n + 128] = hi
                p_lo[2 * k:2 * k + 2, :, zz, :, 128 * n:128 * n + 128] = lo

    y_up, y_down, y_far = lax.rem(row + 2, 8), lax.rem(row + 6, 8), lax.rem(row + 4, 8)
    x_far = row + 1 - 2 * lax.rem(row, 2)

    out_plane, in_plane = sems(0, 2), sems(1, 3 * NCHUNK)

    def plane_copy(u, k, r, to):
        send(x_all.at[u, r, core], x_all.at[u, r, core], out_plane, in_plane + 3 * u + k, (to, col))

    def plane_send(u):
        for to in (y_far, x_far, y_up, y_down):
            plane_copy(u, 0, row, to)

    def plane_pass(u):
        wait_recv(x_all.at[u, 0:4, 0], in_plane + 3 * u)
        plane_copy(u, 1, x_far, y_up)
        plane_copy(u, 1, x_far, y_down)
        if u < 3:
            plane_copy(u, 1, y_far, x_far)
        else:
            plane_copy(u, 1, x_far, y_far)

    def plane_end(u):
        wait_recv(x_all.at[u, 0:3, 0], in_plane + 3 * u + 1)
        send(x_all.at[u, :, core], x_all.at[u, :, core], out_plane + 1, in_plane + 3 * u + 2, sib)

    def plane_wait(u):
        wait_recv(x_all.at[u, :, 0], in_plane + 3 * u + 2)

    out_mid, out_far, in_mid, in_far = sems(0), sems(0), sems(1, NCHUNK), sems(1, NCHUNK)
    out_cross, in_cross = sems(0, 3), sems(1, 3)
    out_g, in_g = sems(0, 2), sems(1, 2)
    out_s, in_s = sems(0, 3), sems(1, 3)

    def sel_send():
        select()
        for d in (4, 5, 3, 2, 6, 7, 1, 0):
            to = lax.rem(row + d, PLANE)
            if d:
                send(sel.at[child], s_all.at[row, core, child], out_s, in_s, (to, col))
            send(sel.at[1 - child], s_all.at[row, core, child], out_s + 1, in_s + 1, at(to, 1 - child, z, core))

    def sel_pass():
        wait_recv(s_all.at[0:7, 0, 0], in_s)
        wait_recv(s_all.at[:, 0, 0], in_s + 1)
        send(s_all.at[:, core], s_all.at[:, core], out_s + 2, in_s + 2, sib)

    def sel_end():
        wait_recv(s_all.at[:, 0], in_s + 2)

    def s_end():
        sel_pass()
        sel_end()
        pos = lax.broadcasted_iota(jnp.int32, (256, 256), 0)
        old = lax.broadcasted_iota(jnp.int32, (256, 256), 1)
        a, k, j, r, u = pos >> 6, (pos >> 5) & 1, (pos >> 4) & 1, (pos >> 1) & 7, pos & 1
        order = jnp.where(old == r * 32 + j * 16 + k * 8 + a * 2 + u, 1.0, 0.0).astype(BF16)
        hi, lo = split(s_all[...].reshape(256, 2048))
        s_cat[0:256] = mm(order, hi).astype(BF16)
        s_cat[256:512] = mm(order, lo).astype(BF16)

    def x_compute(n):
        b_hi, b_lo = k_hi[...].reshape(1024, 128), k_lo[...].reshape(1024, 128)
        parts = []
        for k in range(2):
            x = mm(s_cat[:, 1024 * k:1024 * k + 1024], b_hi)
            parts.append(x[0:256] + (x[256:512] + mm(s_cat[0:256, 1024 * k:1024 * k + 1024], b_lo)))
        x = -(parts[0] + pltpu.roll(parts[1], 64, 1))
        if n % 2:
            x_own[n // 2] = merge(x_own[n // 2].reshape(256, 128), x).reshape(4, 2, 32, 128)
        else:
            x_own[n // 2] = x.reshape(4, 2, 32, 128)
        x_send[n] = x.T[0:64]

        @pl.when(mid_self)
        def _():
            x_mid[n] = x_send[n]

        @pl.when(jnp.logical_not(mid_self))
        def _():
            send(x_send.at[n], x_mid.at[n], out_mid, in_mid + n, (mid_row, col))

    def cross_send(n):
        for k, d in enumerate(QUAD):
            c2, j2 = quad(d)
            send(x_own.at[n, :, c2, pl.ds(pl.multiple_of(16 * j2, 16), 16), :], c_in.at[child, core, n],
                 out_cross + k, in_cross + k, at(row, c2, z, j2))
        c_in[child, core, n] = x_own[n, :, child, pl.ds(pl.multiple_of(16 * core, 16), 16), :]

    def mid_pass(u):
        @pl.when(jnp.logical_not(mid_self))
        def _():
            wait_recv(x_mid.at[u], in_mid + u)

        @pl.when(far_self)
        def _():
            x_all[u, row, core] = x_mid[u]

        @pl.when(jnp.logical_not(far_self))
        def _():
            send(x_mid.at[u], x_all.at[u, row, half2], out_far, in_far + u, far)

    def far_pass(u):
        @pl.when(jnp.logical_not(far_self))
        def _():
            wait_recv(x_all.at[u, 0, 0], in_far + u)
        plane_send(u)

    def plane_slot(zz, h):
        w = bit_xor(h, zz % 2)
        ee = lax.rem(m - zz // 2 - 2 * h + 16, 4)
        return 4 * w + 2 * lax.div(ee, 2) + bit_xor(lax.rem(ee, 2), w)

    def g_compute(u):
        plane_wait(u)
        for rel in range(2):
            h = bit_xor(child, rel)
            for zz in range(8):
                x_hi, x_lo = split(x_all[u, plane_slot(zz, h), h])
                x_cat[64 * rel:64 * rel + 64, 256 * zz:256 * zz + 256] = x_hi
                x_cat[64 * rel + 128:64 * rel + 192, 256 * zz:256 * zz + 256] = x_lo
        b_hi = jnp.concatenate([p_hi[:, :, zz].reshape(256, 384) for zz in range(8)])
        g = mm(x_cat[...], b_hi)
        b_lo = jnp.concatenate([p_lo[:, :, zz].reshape(256, 384) for zz in range(8)])
        g = g[0:128] + (g[128:256] + mm(x_cat[0:128], b_lo))
        g_own[u] = g.reshape(2, 64, 384)

    def g_send(u):
        j2, k = u // 3, u % 3
        send(g_own.at[u, 1], g_in.at[child, core, k], out_g + 1, in_g + 1, at(row, 1 - child, z, j2))

        @pl.when(core == j2)
        def _():
            g_in[child, core, k] = g_own[u, 0]

        @pl.when(core != j2)
        def _():
            send(g_own.at[u, 0], g_in.at[child, core, k], out_g, in_g, sib)

    def cross_write():
        for k in range(3):
            wait_recv(c_in.at[0, 0], in_cross + k)
        for c in range(2):
            for h in range(2):
                for n in range(3):
                    cross[c, :, :, 384 * h + 128 * n:384 * h + 128 * n + 128] = c_in[c, h, n]

    def cov_write():
        loads[2].wait()
        wait_recv(g_in.at[0, 0], in_g)
        wait_recv(g_in.at[0], in_g + 1)
        for c in range(2):
            for h in range(2):
                cov[c, :, 384 * h:384 * h + 384] = inverse[c, :, 384 * h:384 * h + 384] - g_in[c, h].reshape(192, 384)

    quad_send(0)
    quad_send(1)
    quad_send(2)
    sel_send()
    quad_wait(0)
    ring(0, 0)
    ring(1, 0)
    quad_wait(1)
    ring(2, 0)
    ring(0, 1)
    ring(1, 1)
    ring(0, 2)
    ring(2, 1)
    ring(1, 2)
    ring(0, 3)
    quad_wait(2)
    ring(3, 0)
    ring(2, 2)
    ring(1, 3)
    ring(3, 1)
    ring(4, 0)
    s_end()
    ring_end(0)
    x_compute(0)
    ring(2, 3)
    ring(3, 2)
    ring_end(1)
    x_compute(1)
    ring(4, 1)
    ring(5, 0)
    mid_pass(0)
    ring(3, 3)
    ring(4, 2)
    mid_pass(1)
    ring_end(2)
    x_compute(2)
    ring(5, 1)
    ring(4, 3)
    far_pass(0)
    ring_end(3)
    x_compute(3)
    cross_send(0)
    unpack(0)
    ring(5, 2)
    mid_pass(2)
    far_pass(1)
    ring(5, 3)
    plane_pass(0)
    ring_end(4)
    x_compute(4)
    mid_pass(3)
    far_pass(2)
    plane_pass(1)
    ring_end(5)
    x_compute(5)
    mid_pass(4)
    mid_pass(5)
    plane_end(0)
    far_pass(3)
    plane_pass(2)
    plane_end(1)
    far_pass(4)
    plane_pass(3)
    far_pass(5)
    plane_end(2)
    cross_send(1)
    unpack(1)
    unpack(2)
    g_compute(0)
    g_send(0)
    plane_pass(4)
    plane_end(3)
    g_compute(1)
    g_send(1)
    plane_pass(5)
    g_compute(2)
    g_send(2)
    plane_end(4)
    g_compute(3)
    g_send(3)
    cross_send(2)
    g_compute(4)
    g_send(4)
    plane_end(5)
    g_compute(5)
    g_send(5)
    cross_write()
    cov_write()

    for k in range(3):
        wait_send(packed.at[0, 0], out_quad + k)
        wait_send(c_in.at[0, 0], out_cross + k)
    wait_send(s_all.at[0:7, 0, 0], out_s)
    wait_send(s_all.at[:, 0, 0], out_s + 1)
    wait_send(s_all.at[:, 0], out_s + 2)
    wait_send(p_all.at[:, 0:7], out_ring)
    wait_send(x_all.at[:, 0:7, 0], out_plane)
    wait_send(x_all.at[:, :, 0], out_plane + 1)
    wait_send(g_own.at[0:3, 0], out_g)
    wait_send(g_own.at[:, 0], out_g + 1)

    @pl.when(jnp.logical_not(mid_self))
    def _():
        wait_send(x_send, out_mid)

    @pl.when(jnp.logical_not(far_self))
    def _():
        wait_send(x_mid, out_far)


N_OUT, N_IN = 16, 65


def body(top_inverse, normed_panel, child_inverse, structure):
    vmem = pl.BlockSpec(memory_space=pltpu.VMEM)
    panel = normed_panel.reshape(2, 2, 2, 16, 768)
    return pl.pallas_call(
        kernel,
        out_shape=(jax.ShapeDtypeStruct((2, 4, 16, 768), F32), jax.ShapeDtypeStruct((2, 192, 768), F32)),
        in_specs=[pl.BlockSpec(memory_space=pltpu.SMEM)] + [pl.BlockSpec(memory_space=pl.ANY)] * 3,
        out_specs=(vmem, vmem),
        scratch_shapes=[
            pltpu.VMEM((24, 2, 24, 512), F32),
            pltpu.VMEM((2, 2, 2, 16, 768), F32),
            pltpu.VMEM((2, 2, 6, 2, 16, 128), F32),
            pltpu.VMEM((2, 192, 768), F32),
            pltpu.VMEM((2, 8, 2048), F32),
            pltpu.VMEM((8, 2, 2, 8, 2048), F32),
            pltpu.VMEM((512, 2048), BF16),
            pltpu.VMEM((NCHUNK, 8, 2, 2, 32, 128), F32),
            pltpu.VMEM((2, 2, 8, 32, 128), BF16),
            pltpu.VMEM((2, 2, 8, 32, 128), BF16),
            pltpu.VMEM((4, 2, 8, 32, 384), BF16),
            pltpu.VMEM((4, 2, 8, 32, 384), BF16),
            pltpu.VMEM((3, 4, 2, 32, 128), F32),
            pltpu.VMEM((NCHUNK, 64, 256), F32),
            pltpu.VMEM((NCHUNK, 64, 256), F32),
            pltpu.VMEM((NCHUNK, 8, 2, 64, 256), F32),
            pltpu.VMEM((256, 2048), BF16),
            pltpu.VMEM((NCHUNK, 2, 64, 384), F32),
            pltpu.VMEM((2, 2, 3, 64, 384), F32),
            pltpu.VMEM((2, 2, 3, 4, 16, 128), F32),
            pltpu.SemaphoreType.DMA((N_OUT,)),
            pltpu.SemaphoreType.DMA((N_IN,)),
            pltpu.SemaphoreType.DMA((3,)),
        ],
        compiler_params=pltpu.CompilerParams(collective_id=0, has_side_effects=True, vmem_limit_bytes=52 * 2**20),
        name="selected_inverse",
    )(structure, top_inverse, panel, child_inverse)


def solution(mesh):
    in_specs = (
        P(None, ("pcol", "prow"), None, None),
        P(None, None, "pcol", "prow"),
        P(None, "pcol", "prow"),
        P(),
    )
    out_specs = (P(None, None, "pcol", "prow"), P(None, "pcol", "prow"))
    return jax.shard_map(body, mesh=mesh, in_specs=in_specs, out_specs=out_specs, check_vma=False)
```

```python
import functools

import jax
import jax.numpy as jnp
from jax import lax
from jax.experimental import pallas as pl
from jax.experimental.pallas import tpu as pltpu
from jax.sharding import PartitionSpec as P

MESH = pl.DeviceIdType.MESH
F32, BF16 = jnp.float32, jnp.bfloat16
NCHUNK = 6
QUAD = ((0, 1), (1, 0), (1, 1))
PLANE = 8


def bit_xor(a, b):
    return lax.rem(a + b, 2)


def split(x):
    hi = x.astype(BF16)
    return hi, (x - hi.astype(F32)).astype(BF16)


def merge(a, b):
    lane = lax.broadcasted_iota(jnp.int32, a.shape, a.ndim - 1)
    return jnp.where(lane < 64, a, pltpu.roll(b, 64, a.ndim - 1))


def merge_high(a, b):
    lane = lax.broadcasted_iota(jnp.int32, a.shape, a.ndim - 1)
    return jnp.where(lane < 64, pltpu.roll(a, 64, a.ndim - 1), b)


def mm(a, b):
    return jnp.dot(a, b, preferred_element_type=F32)


def kernel(structure, top_hbm, panel_hbm, inverse_hbm, cross, cov, top, panel, packed, inverse, sel, s_all, s_cat, p_all, k_hi, k_lo, p_hi, p_lo,
           x_own, x_send, x_mid, x_all, x_cat, g_own, g_in, c_in, ss, rs, ls):
    row, col = lax.axis_index("prow"), lax.axis_index("pcol")
    child, z, core = lax.div(col, 16), lax.rem(lax.div(col, 2), 8), lax.rem(col, 2)

    def at(r, c, zz, j):
        return (r, (c * 8 + lax.rem(zz + 8, 8)) * 2 + j)

    def quad(d):
        return bit_xor(child, d[0]), bit_xor(core, d[1])

    counts = [0, 0]

    def sems(side, count=1):
        counts[side] += count
        return counts[side] - count

    def send(src, dst, out, into, device):
        pltpu.make_async_remote_copy(src, dst, ss.at[out], rs.at[into], device_id=device, device_id_type=MESH).start()

    def wait_send(ref, index):
        pltpu.make_async_remote_copy(ref, ref, ss.at[index], rs.at[0], device_id=(row, col), device_id_type=MESH).wait_send()

    def wait_recv(ref, index):
        pltpu.make_async_remote_copy(ref, ref, ss.at[0], rs.at[index], device_id=(row, col), device_id_type=MESH).wait_recv()

    sib = at(row, child, z, 1 - core)
    half, quarter = lax.div(row, 4), lax.rem(row, 4)
    m, s = lax.div(z, 2), lax.rem(z, 2)
    sw = bit_xor(half, s)
    e = lax.rem(quarter - m - 2 * half + 8, 4)
    mid_row = 4 * sw + 2 * lax.div(e, 2) + bit_xor(lax.rem(e, 2), sw)
    mid_self = mid_row == row
    sw2 = lax.div(row, 4)
    e2 = 2 * lax.div(quarter, 2) + bit_xor(lax.rem(quarter, 2), sw2)
    half2 = bit_xor(sw2, s)
    q2 = lax.rem(e2 + m + 2 * half2, 4)
    far_z = 2 * q2 + core
    far = at(row, child, far_z, half2)
    far_self = (far_z == z) & (half2 == core)
    half3 = core
    m3 = lax.rem(m - e2 - 2 * half3 + 8, 4)
    s3 = bit_xor(sw2, half3)
    from_z = 2 * m3 + s3
    from_core = s
    src_far = at(row, child, from_z, from_core)

    loads = [pltpu.make_async_copy(a, b, ls.at[i]) for i, (a, b) in enumerate(((panel_hbm, panel), (top_hbm, top), (inverse_hbm, inverse)))]
    for load in loads:
        load.start()
    barrier = pltpu.get_barrier_semaphore()

    def greet(device):
        pl.semaphore_signal(barrier, inc=1, device_id=device, device_id_type=MESH)

    for d in QUAD:
        greet(at(row, quad(d)[0], z, quad(d)[1]))
    greet(at(row, child, z + 1, core))
    greet(at(row, child, z - 1, core))
    for d in range(1, PLANE):
        greet((lax.rem(row + d, PLANE), col))

    @pl.when(jnp.logical_not(far_self))
    def _():
        greet(far)
        greet(src_far)

    loads[0].wait()
    for c in range(2):
        for j in range(2):
            for n in range(3):
                for b in range(2):
                    low = panel[c, 0, b, :, 384 * j + 128 * n:384 * j + 128 * n + 128]
                    high = panel[c, 1, b, :, 384 * j + 128 * n:384 * j + 128 * n + 128]
                    packed[c, j, 2 * n, b] = merge(low, high)
                    packed[c, j, 2 * n + 1, b] = merge_high(low, high)
    for t in range(NCHUNK):
        p_all[t, z, :, child, pl.ds(pl.multiple_of(16 * core, 16), 16), :] = packed[child, core, t]
    def select():
        loads[1].wait()
        for c in range(2):
            for a in range(4):
                for u in range(2):
                    for b in range(4):
                        sel[c, 2 * a + u:2 * a + u + 1, 512 * b:512 * b + 512] = top[structure[c, a], u, pl.ds(structure[c, b], 1), :]
        s_all[row, core, child] = sel[child]

    select()
    pl.semaphore_wait(barrier, 12 + 2 * (1 - far_self.astype(jnp.int32)))

    out_quad, in_quad = sems(0, 3), sems(1, 3)

    def quad_send(n):
        for k, d in enumerate(QUAD):
            c2, j2 = quad(d)
            send(packed.at[c2, j2, 2 * n:2 * n + 2], p_all.at[2 * n:2 * n + 2, z, :, child, pl.ds(pl.multiple_of(16 * core, 16), 16), :],
                 out_quad + k, in_quad + n, at(row, c2, z, j2))

    def quad_wait(n):
        wait_recv(packed.at[0, 0], in_quad + n)

    out_ring, in_ring = sems(0), sems(1, 4 * NCHUNK)

    def chunk(n, zz, part=None):
        ref = p_all.at[n, lax.rem(zz + 16, 8)]
        return ref if part is None else ref.at[part]

    def ring_wait(n, step):
        wait_recv(p_all.at[n, 0:2 if step < 3 else 1], in_ring + 4 * n + step)

    def ring(n, step):
        if step:
            ring_wait(n, step - 1)
        for side, part in ((1, 0), (-1, 1)):
            block = chunk(n, z - side * step, part if step == 3 else None)
            send(block, block, out_ring, in_ring + 4 * n + step, at(row, child, z + side, core))

    def ring_end(n):
        ring_wait(n, 3)
        for zz in range(8):
            k_hi[:, :, zz], k_lo[:, :, zz] = split(p_all[n, zz])

    def unpack(n):
        for zz in range(8):
            even, odd = p_all[2 * n, zz], p_all[2 * n + 1, zz]
            for k, block in enumerate((merge(even, odd), merge_high(even, odd))):
                hi, lo = split(block)
                p_hi[2 * k:2 * k + 2, :, zz, :, 128 * n:128 * n + 128] = hi
                p_lo[2 * k:2 * k + 2, :, zz, :, 128 * n:128 * n + 128] = lo

    y_up, y_down, y_far = lax.rem(row + 2, 8), lax.rem(row + 6, 8), lax.rem(row + 4, 8)
    x_far = row + 1 - 2 * lax.rem(row, 2)

    out_plane, in_plane = sems(0, 2), sems(1, 3 * NCHUNK)

    def plane_copy(u, k, r, to):
        send(x_all.at[u, r, core], x_all.at[u, r, core], out_plane, in_plane + 3 * u + k, (to, col))

    def plane_send(u):
        for to in (y_far, x_far, y_up, y_down):
            plane_copy(u, 0, row, to)

    def plane_pass(u):
        wait_recv(x_all.at[u, 0:4, 0], in_plane + 3 * u)
        plane_copy(u, 1, x_far, y_up)
        plane_copy(u, 1, x_far, y_down)
        plane_copy(u, 1, y_far, x_far)

    def plane_end(u):
        wait_recv(x_all.at[u, 0:3, 0], in_plane + 3 * u + 1)
        send(x_all.at[u, :, core], x_all.at[u, :, core], out_plane + 1, in_plane + 3 * u + 2, sib)

    def plane_wait(u):
        wait_recv(x_all.at[u, :, 0], in_plane + 3 * u + 2)

    out_mid, out_far, in_mid, in_far = sems(0), sems(0), sems(1, NCHUNK), sems(1, NCHUNK)
    out_cross, in_cross = sems(0, 3), sems(1, 3)
    out_g, in_g = sems(0, 2), sems(1, 2)
    out_s, in_s = sems(0, 3), sems(1, 4)

    def sel_copy(k, r, to):
        send(s_all.at[r, core], s_all.at[r, core], out_s + 1, in_s + k, (to, col))

    def sel_send():
        send(sel.at[1 - child], s_all.at[row, core, child], out_s, in_s, at(row, 1 - child, z, core))

    def sel_spread():
        wait_recv(s_all.at[0, 0, 0], in_s)
        for to in (y_far, x_far, y_up, y_down):
            sel_copy(1, row, to)

    def sel_pass():
        wait_recv(s_all.at[0:4, 0], in_s + 1)
        sel_copy(2, x_far, y_up)
        sel_copy(2, x_far, y_down)
        sel_copy(2, y_far, x_far)

    def sel_join():
        wait_recv(s_all.at[0:3, 0], in_s + 2)
        send(s_all.at[:, core], s_all.at[:, core], out_s + 2, in_s + 3, sib)

    def sel_end():
        wait_recv(s_all.at[:, 0], in_s + 3)

    def s_end():
        sel_join()
        sel_end()
        pos = lax.broadcasted_iota(jnp.int32, (256, 256), 0)
        old = lax.broadcasted_iota(jnp.int32, (256, 256), 1)
        a, k, j, r, u = pos >> 6, (pos >> 5) & 1, (pos >> 4) & 1, (pos >> 1) & 7, pos & 1
        order = jnp.where(old == r * 32 + j * 16 + k * 8 + a * 2 + u, 1.0, 0.0).astype(BF16)
        hi, lo = split(s_all[...].reshape(256, 2048))
        s_cat[0:256] = mm(order, hi).astype(BF16)
        s_cat[256:512] = mm(order, lo).astype(BF16)

    def x_compute(n):
        b_hi, b_lo = k_hi[...].reshape(1024, 128), k_lo[...].reshape(1024, 128)
        parts = []
        for k in range(2):
            x = mm(s_cat[:, 1024 * k:1024 * k + 1024], b_hi)
            parts.append(x[0:256] + (x[256:512] + mm(s_cat[0:256, 1024 * k:1024 * k + 1024], b_lo)))
        x = -(parts[0] + pltpu.roll(parts[1], 64, 1))
        if n % 2:
            x_own[n // 2] = merge(x_own[n // 2].reshape(256, 128), x).reshape(4, 2, 32, 128)
        else:
            x_own[n // 2] = x.reshape(4, 2, 32, 128)
        x_send[n] = x.T[0:64]

        @pl.when(mid_self)
        def _():
            x_mid[n] = x_send[n]

        @pl.when(jnp.logical_not(mid_self))
        def _():
            send(x_send.at[n], x_mid.at[n], out_mid, in_mid + n, (mid_row, col))

    def cross_send(n):
        for k, d in enumerate(QUAD):
            c2, j2 = quad(d)
            send(x_own.at[n, :, c2, pl.ds(pl.multiple_of(16 * j2, 16), 16), :], c_in.at[child, core, n],
                 out_cross + k, in_cross + k, at(row, c2, z, j2))
        c_in[child, core, n] = x_own[n, :, child, pl.ds(pl.multiple_of(16 * core, 16), 16), :]

    def mid_pass(u):
        @pl.when(jnp.logical_not(mid_self))
        def _():
            wait_recv(x_mid.at[u], in_mid + u)

        @pl.when(far_self)
        def _():
            x_all[u, row, core] = x_mid[u]

        @pl.when(jnp.logical_not(far_self))
        def _():
            send(x_mid.at[u], x_all.at[u, row, half2], out_far, in_far + u, far)

    def far_pass(u):
        @pl.when(jnp.logical_not(far_self))
        def _():
            wait_recv(x_all.at[u, 0, 0], in_far + u)
        plane_send(u)

    def plane_slot(zz, h):
        w = bit_xor(h, zz % 2)
        ee = lax.rem(m - zz // 2 - 2 * h + 16, 4)
        return 4 * w + 2 * lax.div(ee, 2) + bit_xor(lax.rem(ee, 2), w)

    def g_compute(u):
        plane_wait(u)
        for rel in range(2):
            h = bit_xor(child, rel)
            for zz in range(8):
                x_hi, x_lo = split(x_all[u, plane_slot(zz, h), h])
                x_cat[64 * rel:64 * rel + 64, 256 * zz:256 * zz + 256] = x_hi
                x_cat[64 * rel + 128:64 * rel + 192, 256 * zz:256 * zz + 256] = x_lo
        b_hi = jnp.concatenate([p_hi[:, :, zz].reshape(256, 384) for zz in range(8)])
        g = mm(x_cat[...], b_hi)
        b_lo = jnp.concatenate([p_lo[:, :, zz].reshape(256, 384) for zz in range(8)])
        g = g[0:128] + (g[128:256] + mm(x_cat[0:128], b_lo))
        g_own[u] = g.reshape(2, 64, 384)

    def g_send(u):
        j2, k = u // 3, u % 3
        send(g_own.at[u, 1], g_in.at[child, core, k], out_g + 1, in_g + 1, at(row, 1 - child, z, j2))

        @pl.when(core == j2)
        def _():
            g_in[child, core, k] = g_own[u, 0]

        @pl.when(core != j2)
        def _():
            send(g_own.at[u, 0], g_in.at[child, core, k], out_g, in_g, sib)

    def cross_write():
        for k in range(3):
            wait_recv(c_in.at[0, 0], in_cross + k)
        for c in range(2):
            for h in range(2):
                for n in range(3):
                    cross[c, :, :, 384 * h + 128 * n:384 * h + 128 * n + 128] = c_in[c, h, n]

    def cov_write():
        loads[2].wait()
        wait_recv(g_in.at[0, 0], in_g)
        wait_recv(g_in.at[0], in_g + 1)
        for c in range(2):
            for h in range(2):
                cov[c, :, 384 * h:384 * h + 384] = inverse[c, :, 384 * h:384 * h + 384] - g_in[c, h].reshape(192, 384)

    quad_send(0)
    sel_send()
    quad_send(1)
    quad_send(2)
    quad_wait(0)
    ring(0, 0)
    ring(1, 0)
    sel_spread()
    quad_wait(1)
    ring(2, 0)
    ring(0, 1)
    ring(1, 1)
    ring(0, 2)
    ring(2, 1)
    ring(1, 2)
    sel_pass()
    ring(0, 3)
    quad_wait(2)
    ring(3, 0)
    ring(2, 2)
    ring(1, 3)
    ring(3, 1)
    ring(4, 0)
    s_end()
    ring_end(0)
    x_compute(0)
    ring(2, 3)
    ring(3, 2)
    ring_end(1)
    x_compute(1)
    ring(4, 1)
    ring(5, 0)
    mid_pass(0)
    ring(3, 3)
    ring(4, 2)
    mid_pass(1)
    ring_end(2)
    x_compute(2)
    ring(5, 1)
    ring(4, 3)
    far_pass(0)
    ring_end(3)
    x_compute(3)
    cross_send(0)
    unpack(0)
    ring(5, 2)
    mid_pass(2)
    far_pass(1)
    ring(5, 3)
    plane_pass(0)
    ring_end(4)
    x_compute(4)
    mid_pass(3)
    far_pass(2)
    plane_pass(1)
    ring_end(5)
    x_compute(5)
    mid_pass(4)
    mid_pass(5)
    plane_end(0)
    far_pass(3)
    plane_pass(2)
    plane_end(1)
    far_pass(4)
    plane_pass(3)
    far_pass(5)
    plane_end(2)
    cross_send(1)
    unpack(1)
    unpack(2)
    g_compute(0)
    g_send(0)
    plane_pass(4)
    plane_end(3)
    g_compute(1)
    g_send(1)
    plane_pass(5)
    g_compute(2)
    g_send(2)
    plane_end(4)
    g_compute(3)
    g_send(3)
    cross_send(2)
    g_compute(4)
    g_send(4)
    plane_end(5)
    g_compute(5)
    g_send(5)
    cross_write()
    cov_write()

    for k in range(3):
        wait_send(packed.at[0, 0], out_quad + k)
        wait_send(c_in.at[0, 0], out_cross + k)
    wait_send(s_all.at[0, 0, 0], out_s)
    wait_send(s_all.at[0:7, 0], out_s + 1)
    wait_send(s_all.at[:, 0], out_s + 2)
    wait_send(p_all.at[:, 0:7], out_ring)
    wait_send(x_all.at[:, 0:7, 0], out_plane)
    wait_send(x_all.at[:, :, 0], out_plane + 1)
    wait_send(g_own.at[0:3, 0], out_g)
    wait_send(g_own.at[:, 0], out_g + 1)

    @pl.when(jnp.logical_not(mid_self))
    def _():
        wait_send(x_send, out_mid)

    @pl.when(jnp.logical_not(far_self))
    def _():
        wait_send(x_mid, out_far)


N_OUT, N_IN = 16, 66


def body(top_inverse, normed_panel, child_inverse, structure):
    vmem = pl.BlockSpec(memory_space=pltpu.VMEM)
    panel = normed_panel.reshape(2, 2, 2, 16, 768)
    return pl.pallas_call(
        kernel,
        out_shape=(jax.ShapeDtypeStruct((2, 4, 16, 768), F32), jax.ShapeDtypeStruct((2, 192, 768), F32)),
        in_specs=[pl.BlockSpec(memory_space=pltpu.SMEM)] + [pl.BlockSpec(memory_space=pl.ANY)] * 3,
        out_specs=(vmem, vmem),
        scratch_shapes=[
            pltpu.VMEM((24, 2, 24, 512), F32),
            pltpu.VMEM((2, 2, 2, 16, 768), F32),
            pltpu.VMEM((2, 2, 6, 2, 16, 128), F32),
            pltpu.VMEM((2, 192, 768), F32),
            pltpu.VMEM((2, 8, 2048), F32),
            pltpu.VMEM((8, 2, 2, 8, 2048), F32),
            pltpu.VMEM((512, 2048), BF16),
            pltpu.VMEM((NCHUNK, 8, 2, 2, 32, 128), F32),
            pltpu.VMEM((2, 2, 8, 32, 128), BF16),
            pltpu.VMEM((2, 2, 8, 32, 128), BF16),
            pltpu.VMEM((4, 2, 8, 32, 384), BF16),
            pltpu.VMEM((4, 2, 8, 32, 384), BF16),
            pltpu.VMEM((3, 4, 2, 32, 128), F32),
            pltpu.VMEM((NCHUNK, 64, 256), F32),
            pltpu.VMEM((NCHUNK, 64, 256), F32),
            pltpu.VMEM((NCHUNK, 8, 2, 64, 256), F32),
            pltpu.VMEM((256, 2048), BF16),
            pltpu.VMEM((NCHUNK, 2, 64, 384), F32),
            pltpu.VMEM((2, 2, 3, 64, 384), F32),
            pltpu.VMEM((2, 2, 3, 4, 16, 128), F32),
            pltpu.SemaphoreType.DMA((N_OUT,)),
            pltpu.SemaphoreType.DMA((N_IN,)),
            pltpu.SemaphoreType.DMA((3,)),
        ],
        compiler_params=pltpu.CompilerParams(collective_id=0, has_side_effects=True, vmem_limit_bytes=52 * 2**20),
        name="selected_inverse",
    )(structure, top_inverse, panel, child_inverse)


def solution(mesh):
    in_specs = (
        P(None, ("pcol", "prow"), None, None),
        P(None, None, "pcol", "prow"),
        P(None, "pcol", "prow"),
        P(),
    )
    out_specs = (P(None, None, "pcol", "prow"), P(None, "pcol", "prow"))
    return jax.shard_map(body, mesh=mesh, in_specs=in_specs, out_specs=out_specs, check_vma=False)
```

```python
import functools

import jax
import jax.numpy as jnp
from jax import lax
from jax.experimental import pallas as pl
from jax.experimental.pallas import tpu as pltpu
from jax.sharding import PartitionSpec as P

MESH = pl.DeviceIdType.MESH
F32, BF16 = jnp.float32, jnp.bfloat16
NCHUNK = 6
QUAD = ((0, 1), (1, 0), (1, 1))
PLANE = 8


def bit_xor(a, b):
    return lax.rem(a + b, 2)


def split(x):
    hi = x.astype(BF16)
    return hi, (x - hi.astype(F32)).astype(BF16)


def merge(a, b):
    lane = lax.broadcasted_iota(jnp.int32, a.shape, a.ndim - 1)
    return jnp.where(lane < 64, a, pltpu.roll(b, 64, a.ndim - 1))


def merge_high(a, b):
    lane = lax.broadcasted_iota(jnp.int32, a.shape, a.ndim - 1)
    return jnp.where(lane < 64, pltpu.roll(a, 64, a.ndim - 1), b)


def mm(a, b):
    return jnp.dot(a, b, preferred_element_type=F32)


def kernel(structure, top_hbm, panel_hbm, inverse_hbm, cross, cov, top, panel, packed, inverse, sel, s_all, s_cat, p_all, k_all, p_split,
           x_own, x_send, x_mid, x_all, x_cat, g_own, g_in, c_in, ss, rs, ls):
    row, col = lax.axis_index("prow"), lax.axis_index("pcol")
    child, z, core = lax.div(col, 16), lax.rem(lax.div(col, 2), 8), lax.rem(col, 2)

    def at(r, c, zz, j):
        return (r, (c * 8 + lax.rem(zz + 8, 8)) * 2 + j)

    def quad(d):
        return bit_xor(child, d[0]), bit_xor(core, d[1])

    counts = [0, 0]

    def sems(side, count=1):
        counts[side] += count
        return counts[side] - count

    def send(src, dst, out, into, device):
        pltpu.make_async_remote_copy(src, dst, ss.at[out], rs.at[into], device_id=device, device_id_type=MESH).start()

    def wait_send(ref, index):
        pltpu.make_async_remote_copy(ref, ref, ss.at[index], rs.at[0], device_id=(row, col), device_id_type=MESH).wait_send()

    def wait_recv(ref, index):
        pltpu.make_async_remote_copy(ref, ref, ss.at[0], rs.at[index], device_id=(row, col), device_id_type=MESH).wait_recv()

    sib = at(row, child, z, 1 - core)
    half, quarter = lax.div(row, 4), lax.rem(row, 4)
    m, s = lax.div(z, 2), lax.rem(z, 2)
    sw = bit_xor(half, s)
    e = lax.rem(quarter - m - 2 * half + 8, 4)
    mid_row = 4 * sw + 2 * lax.div(e, 2) + bit_xor(lax.rem(e, 2), sw)
    mid_self = mid_row == row
    sw2 = lax.div(row, 4)
    e2 = 2 * lax.div(quarter, 2) + bit_xor(lax.rem(quarter, 2), sw2)
    half2 = bit_xor(sw2, s)
    q2 = lax.rem(e2 + m + 2 * half2, 4)
    far_z = 2 * q2 + core
    far = at(row, child, far_z, half2)
    far_self = (far_z == z) & (half2 == core)
    half3 = core
    m3 = lax.rem(m - e2 - 2 * half3 + 8, 4)
    s3 = bit_xor(sw2, half3)
    from_z = 2 * m3 + s3
    from_core = s
    src_far = at(row, child, from_z, from_core)

    loads = [pltpu.make_async_copy(a, b, ls.at[i]) for i, (a, b) in enumerate(((panel_hbm, panel), (top_hbm, top), (inverse_hbm, inverse)))]
    for load in loads:
        load.start()
    barrier = pltpu.get_barrier_semaphore()

    def greet(device):
        pl.semaphore_signal(barrier, inc=1, device_id=device, device_id_type=MESH)

    for d in QUAD:
        greet(at(row, quad(d)[0], z, quad(d)[1]))
    greet(at(row, child, z + 1, core))
    greet(at(row, child, z - 1, core))
    for d in range(1, PLANE):
        greet((lax.rem(row + d, PLANE), col))

    @pl.when(jnp.logical_not(far_self))
    def _():
        greet(far)
        greet(src_far)

    loads[0].wait()
    for c in range(2):
        for j in range(2):
            for n in range(3):
                for b in range(2):
                    low = panel[c, 0, b, :, 384 * j + 128 * n:384 * j + 128 * n + 128]
                    high = panel[c, 1, b, :, 384 * j + 128 * n:384 * j + 128 * n + 128]
                    packed[c, j, 2 * n, b] = merge(low, high)
                    packed[c, j, 2 * n + 1, b] = merge_high(low, high)
    for t in range(NCHUNK):
        p_all[t, z, :, child, pl.ds(pl.multiple_of(16 * core, 16), 16), :] = packed[child, core, t]
    def select():
        loads[1].wait()
        for c in range(2):
            for a in range(4):
                for u in range(2):
                    for b in range(4):
                        sel[c, 2 * a + u:2 * a + u + 1, 512 * b:512 * b + 512] = top[structure[c, a], u, pl.ds(structure[c, b], 1), :]
        s_all[row, core, child] = sel[child]

    select()
    pl.semaphore_wait(barrier, 12 + 2 * (1 - far_self.astype(jnp.int32)))

    out_quad, in_quad = sems(0, 3), sems(1, 3)

    def quad_send(n):
        for k, d in enumerate(QUAD):
            c2, j2 = quad(d)
            send(packed.at[c2, j2, 2 * n:2 * n + 2], p_all.at[2 * n:2 * n + 2, z, :, child, pl.ds(pl.multiple_of(16 * core, 16), 16), :],
                 out_quad + k, in_quad + n, at(row, c2, z, j2))

    def quad_wait(n):
        wait_recv(packed.at[0, 0], in_quad + n)

    out_ring, in_ring = sems(0), sems(1, 4 * NCHUNK)

    def chunk(n, zz, part=None):
        ref = p_all.at[n, lax.rem(zz + 16, 8)]
        return ref if part is None else ref.at[part]

    def ring_wait(n, step):
        wait_recv(p_all.at[n, 0:2 if step < 3 else 1], in_ring + 4 * n + step)

    def ring(n, step):
        if step:
            ring_wait(n, step - 1)
        for side, part in ((1, 0), (-1, 1)):
            block = chunk(n, z - side * step, part if step == 3 else None)
            send(block, block, out_ring, in_ring + 4 * n + step, at(row, child, z + side, core))

    def ring_end(n):
        ring_wait(n, 3)
        for zz in range(8):
            k_all[:, :, zz, :, 0:128], k_all[:, :, zz, :, 128:256] = split(p_all[n, zz])

    def unpack(n):
        for zz in range(8):
            even, odd = p_all[2 * n, zz], p_all[2 * n + 1, zz]
            for k, block in enumerate((merge(even, odd), merge_high(even, odd))):
                hi, lo = split(block)
                p_split[2 * k:2 * k + 2, :, zz, :, 128 * n:128 * n + 128] = hi
                p_split[2 * k:2 * k + 2, :, zz, :, 384 + 128 * n:512 + 128 * n] = lo

    y_up, y_down, y_far = lax.rem(row + 2, 8), lax.rem(row + 6, 8), lax.rem(row + 4, 8)
    x_far = row + 1 - 2 * lax.rem(row, 2)

    out_plane, in_plane = sems(0, 2), sems(1, 3 * NCHUNK)

    def plane_copy(u, k, r, to):
        send(x_all.at[u, r, core], x_all.at[u, r, core], out_plane, in_plane + 3 * u + k, (to, col))

    def plane_send(u):
        for to in (y_far, x_far, y_up, y_down):
            plane_copy(u, 0, row, to)

    def plane_pass(u):
        wait_recv(x_all.at[u, 0:4, 0], in_plane + 3 * u)
        plane_copy(u, 1, x_far, y_up)
        plane_copy(u, 1, x_far, y_down)
        plane_copy(u, 1, y_far, x_far)

    def plane_end(u):
        wait_recv(x_all.at[u, 0:3, 0], in_plane + 3 * u + 1)
        send(x_all.at[u, :, core], x_all.at[u, :, core], out_plane + 1, in_plane + 3 * u + 2, sib)

    def plane_wait(u):
        wait_recv(x_all.at[u, :, 0], in_plane + 3 * u + 2)

    out_mid, out_far, in_mid, in_far = sems(0), sems(0), sems(1, NCHUNK), sems(1, NCHUNK)
    out_cross, in_cross = sems(0, 3), sems(1, 3)
    out_g, in_g = sems(0, 2), sems(1, 2)
    out_s, in_s = sems(0, 3), sems(1, 4)

    def sel_copy(k, r, to):
        send(s_all.at[r, core], s_all.at[r, core], out_s + 1, in_s + k, (to, col))

    def sel_send():
        send(sel.at[1 - child], s_all.at[row, core, child], out_s, in_s, at(row, 1 - child, z, core))

    def sel_spread():
        wait_recv(s_all.at[0, 0, 0], in_s)
        for to in (y_far, x_far, y_up, y_down):
            sel_copy(1, row, to)

    def sel_pass():
        wait_recv(s_all.at[0:4, 0], in_s + 1)
        sel_copy(2, x_far, y_up)
        sel_copy(2, x_far, y_down)
        sel_copy(2, y_far, x_far)

    def sel_join():
        wait_recv(s_all.at[0:3, 0], in_s + 2)
        send(s_all.at[:, core], s_all.at[:, core], out_s + 2, in_s + 3, sib)

    def sel_end():
        wait_recv(s_all.at[:, 0], in_s + 3)

    def s_end():
        sel_join()
        sel_end()
        pos = lax.broadcasted_iota(jnp.int32, (256, 256), 0)
        old = lax.broadcasted_iota(jnp.int32, (256, 256), 1)
        a, k, j, r, u = pos >> 6, (pos >> 5) & 1, (pos >> 4) & 1, (pos >> 1) & 7, pos & 1
        order = jnp.where(old == r * 32 + j * 16 + k * 8 + a * 2 + u, 1.0, 0.0).astype(BF16)
        hi, lo = split(s_all[...].reshape(256, 2048))
        s_cat[0:256] = mm(order, hi).astype(BF16)
        s_cat[256:512] = mm(order, lo).astype(BF16)

    def x_compute(n):
        b = k_all[...].reshape(1024, 256)
        parts = []
        for k in range(2):
            x = mm(s_cat[:, 1024 * k:1024 * k + 1024], b)
            parts.append(x[0:256, 0:128] + (x[256:512, 0:128] + x[0:256, 128:256]))
        x = -(parts[0] + pltpu.roll(parts[1], 64, 1))
        if n % 2:
            x_own[n // 2] = merge(x_own[n // 2].reshape(256, 128), x).reshape(4, 2, 32, 128)
        else:
            x_own[n // 2] = x.reshape(4, 2, 32, 128)
        x_send[n] = x.T[0:64]

        @pl.when(mid_self)
        def _():
            x_mid[n] = x_send[n]

        @pl.when(jnp.logical_not(mid_self))
        def _():
            send(x_send.at[n], x_mid.at[n], out_mid, in_mid + n, (mid_row, col))

    def cross_send(n):
        for k, d in enumerate(QUAD):
            c2, j2 = quad(d)
            send(x_own.at[n, :, c2, pl.ds(pl.multiple_of(16 * j2, 16), 16), :], c_in.at[child, core, n],
                 out_cross + k, in_cross + k, at(row, c2, z, j2))
        c_in[child, core, n] = x_own[n, :, child, pl.ds(pl.multiple_of(16 * core, 16), 16), :]

    def mid_pass(u):
        @pl.when(jnp.logical_not(mid_self))
        def _():
            wait_recv(x_mid.at[u], in_mid + u)

        @pl.when(far_self)
        def _():
            x_all[u, row, core] = x_mid[u]

        @pl.when(jnp.logical_not(far_self))
        def _():
            send(x_mid.at[u], x_all.at[u, row, half2], out_far, in_far + u, far)

    def far_pass(u):
        @pl.when(jnp.logical_not(far_self))
        def _():
            wait_recv(x_all.at[u, 0, 0], in_far + u)
        plane_send(u)

    def plane_slot(zz, h):
        w = bit_xor(h, zz % 2)
        ee = lax.rem(m - zz // 2 - 2 * h + 16, 4)
        return 4 * w + 2 * lax.div(ee, 2) + bit_xor(lax.rem(ee, 2), w)

    def g_compute(u):
        plane_wait(u)
        for rel in range(2):
            h = bit_xor(child, rel)
            for zz in range(8):
                x_hi, x_lo = split(x_all[u, plane_slot(zz, h), h])
                x_cat[64 * rel:64 * rel + 64, 256 * zz:256 * zz + 256] = x_hi
                x_cat[64 * rel + 128:64 * rel + 192, 256 * zz:256 * zz + 256] = x_lo
        g = mm(x_cat[...], jnp.concatenate([p_split[:, :, zz].reshape(256, 768) for zz in range(8)]))
        g = g[0:128, 0:384] + (g[128:256, 0:384] + g[0:128, 384:768])
        g_own[u] = g.reshape(2, 64, 384)

    def g_send(u):
        j2, k = u // 3, u % 3
        send(g_own.at[u, 1], g_in.at[child, core, k], out_g + 1, in_g + 1, at(row, 1 - child, z, j2))

        @pl.when(core == j2)
        def _():
            g_in[child, core, k] = g_own[u, 0]

        @pl.when(core != j2)
        def _():
            send(g_own.at[u, 0], g_in.at[child, core, k], out_g, in_g, sib)

    def cross_write():
        for k in range(3):
            wait_recv(c_in.at[0, 0], in_cross + k)
        for c in range(2):
            for h in range(2):
                for n in range(3):
                    cross[c, :, :, 384 * h + 128 * n:384 * h + 128 * n + 128] = c_in[c, h, n]

    def cov_write():
        loads[2].wait()
        wait_recv(g_in.at[0, 0], in_g)
        wait_recv(g_in.at[0], in_g + 1)
        for c in range(2):
            for h in range(2):
                cov[c, :, 384 * h:384 * h + 384] = inverse[c, :, 384 * h:384 * h + 384] - g_in[c, h].reshape(192, 384)

    quad_send(0)
    sel_send()
    quad_send(1)
    quad_send(2)
    quad_wait(0)
    ring(0, 0)
    ring(1, 0)
    sel_spread()
    quad_wait(1)
    ring(2, 0)
    ring(0, 1)
    ring(1, 1)
    ring(0, 2)
    ring(2, 1)
    ring(1, 2)
    sel_pass()
    ring(0, 3)
    quad_wait(2)
    ring(3, 0)
    ring(2, 2)
    ring(1, 3)
    ring(3, 1)
    ring(4, 0)
    s_end()
    ring_end(0)
    x_compute(0)
    ring(2, 3)
    ring(3, 2)
    ring_end(1)
    x_compute(1)
    ring(4, 1)
    ring(5, 0)
    mid_pass(0)
    ring(3, 3)
    ring(4, 2)
    mid_pass(1)
    ring_end(2)
    x_compute(2)
    ring(5, 1)
    ring(4, 3)
    far_pass(0)
    ring_end(3)
    x_compute(3)
    cross_send(0)
    unpack(0)
    ring(5, 2)
    mid_pass(2)
    far_pass(1)
    ring(5, 3)
    plane_pass(0)
    ring_end(4)
    x_compute(4)
    mid_pass(3)
    far_pass(2)
    plane_pass(1)
    ring_end(5)
    x_compute(5)
    mid_pass(4)
    mid_pass(5)
    plane_end(0)
    far_pass(3)
    plane_pass(2)
    plane_end(1)
    far_pass(4)
    plane_pass(3)
    far_pass(5)
    plane_end(2)
    cross_send(1)
    unpack(1)
    unpack(2)
    g_compute(0)
    g_send(0)
    plane_pass(4)
    plane_end(3)
    g_compute(1)
    g_send(1)
    plane_pass(5)
    g_compute(2)
    g_send(2)
    plane_end(4)
    g_compute(3)
    g_send(3)
    cross_send(2)
    g_compute(4)
    g_send(4)
    plane_end(5)
    g_compute(5)
    g_send(5)
    cross_write()
    cov_write()

    for k in range(3):
        wait_send(packed.at[0, 0], out_quad + k)
        wait_send(c_in.at[0, 0], out_cross + k)
    wait_send(s_all.at[0, 0, 0], out_s)
    wait_send(s_all.at[0:7, 0], out_s + 1)
    wait_send(s_all.at[:, 0], out_s + 2)
    wait_send(p_all.at[:, 0:7], out_ring)
    wait_send(x_all.at[:, 0:7, 0], out_plane)
    wait_send(x_all.at[:, :, 0], out_plane + 1)
    wait_send(g_own.at[0:3, 0], out_g)
    wait_send(g_own.at[:, 0], out_g + 1)

    @pl.when(jnp.logical_not(mid_self))
    def _():
        wait_send(x_send, out_mid)

    @pl.when(jnp.logical_not(far_self))
    def _():
        wait_send(x_mid, out_far)


N_OUT, N_IN = 16, 66


def body(top_inverse, normed_panel, child_inverse, structure):
    vmem = pl.BlockSpec(memory_space=pltpu.VMEM)
    panel = normed_panel.reshape(2, 2, 2, 16, 768)
    return pl.pallas_call(
        kernel,
        out_shape=(jax.ShapeDtypeStruct((2, 4, 16, 768), F32), jax.ShapeDtypeStruct((2, 192, 768), F32)),
        in_specs=[pl.BlockSpec(memory_space=pltpu.SMEM)] + [pl.BlockSpec(memory_space=pl.ANY)] * 3,
        out_specs=(vmem, vmem),
        scratch_shapes=[
            pltpu.VMEM((24, 2, 24, 512), F32),
            pltpu.VMEM((2, 2, 2, 16, 768), F32),
            pltpu.VMEM((2, 2, 6, 2, 16, 128), F32),
            pltpu.VMEM((2, 192, 768), F32),
            pltpu.VMEM((2, 8, 2048), F32),
            pltpu.VMEM((8, 2, 2, 8, 2048), F32),
            pltpu.VMEM((512, 2048), BF16),
            pltpu.VMEM((NCHUNK, 8, 2, 2, 32, 128), F32),
            pltpu.VMEM((2, 2, 8, 32, 256), BF16),
            pltpu.VMEM((4, 2, 8, 32, 768), BF16),
            pltpu.VMEM((3, 4, 2, 32, 128), F32),
            pltpu.VMEM((NCHUNK, 64, 256), F32),
            pltpu.VMEM((NCHUNK, 64, 256), F32),
            pltpu.VMEM((NCHUNK, 8, 2, 64, 256), F32),
            pltpu.VMEM((256, 2048), BF16),
            pltpu.VMEM((NCHUNK, 2, 64, 384), F32),
            pltpu.VMEM((2, 2, 3, 64, 384), F32),
            pltpu.VMEM((2, 2, 3, 4, 16, 128), F32),
            pltpu.SemaphoreType.DMA((N_OUT,)),
            pltpu.SemaphoreType.DMA((N_IN,)),
            pltpu.SemaphoreType.DMA((3,)),
        ],
        compiler_params=pltpu.CompilerParams(collective_id=0, has_side_effects=True, vmem_limit_bytes=52 * 2**20),
        name="selected_inverse",
    )(structure, top_inverse, panel, child_inverse)


def solution(mesh):
    in_specs = (
        P(None, ("pcol", "prow"), None, None),
        P(None, None, "pcol", "prow"),
        P(None, "pcol", "prow"),
        P(),
    )
    out_specs = (P(None, None, "pcol", "prow"), P(None, "pcol", "prow"))
    return jax.shard_map(body, mesh=mesh, in_specs=in_specs, out_specs=out_specs, check_vma=False)
```
